32 devices in a mesh: box: 4 (over z), slab: 8 (over y, x, core).
Axes of the slice: x: 2, y: 2, z: 4, core: 2. Of those that a mesh axis runs over, the one named last changes fastest.
Arguments:
- hidden_field: bfloat16 [4, 8, 64, 128, 128], P('box', None, 'slab'), may hold values from -6 to 6
- cone_grad: float32 [256, 128, 128], P(('box', 'slab')), may hold values from -6 to 6
- conv_weight: bfloat16 [8, 27], replicated, may hold values from -0.4375 to 0.4375
- box_lower: int32 [256], P(('box', 'slab')), may hold values from 0 to 3, as said below
- box_upper: int32 [256], P(('box', 'slab')), may hold values from 0 to 3, as said below
- plane_lower: int32 [256], P(('box', 'slab')), may hold values from 0 to 63, as said below
- plane_upper: int32 [256], P(('box', 'slab')), may hold values from 0 to 63, as said below
- weight_lower: int32 [256], P(('box', 'slab')), may hold values from 0 to 256
- weight_upper: int32 [256], P(('box', 'slab')), may hold values from 0 to 256, as said below
Outputs:
- hidden_grad: bfloat16 [4, 8, 64, 128, 128], P('box', None, 'slab')
- weight_grad: float32 [8, 27], replicated
The draws below stay inside these ranges and needn't reach their ends.
Inputs may be any that keep to these rules, and one draw needn't show every extreme that they name: With g = l // 64 the group of plane l, box_lower[l] is g or g - 1 (never below 0). box_upper[l] = min(box_lower[l] + 1, 3). Each box b has one offset o_b, and for one box, drawn from the seed, o_b = 32; plane_lower[l] = (l + o_b) mod 64 with b = box_lower[l]. plane_upper[l] = (l + o_b) mod 64 with b = box_upper[l], the same offsets. weight_upper[l] = 256 - weight_lower[l].
All inputs are finite; a program needn't handle non-finite values.
Results may differ from the reference program's by a relative error of at most 0.005.
Values may be sent and summed in bfloat16 or wider, within the bound.
A program may use at most 320 MiB of HBM per device.

```python
import jax
import jax.numpy as jnp
from jax import lax

CH = 8
WDEN = 256
NX = 128
NY = 128
NZ = 64
NBOX = 4
NLC = 256


def routing(key):
    base = jax.random.fold_in(key, 11)
    keys = jax.random.split(base, 4)
    offsets = jax.random.randint(keys[0], (NBOX,), 0, NZ).astype(jnp.int32)
    chosen = jax.random.randint(keys[3], (), 0, NBOX).astype(jnp.int32)
    offsets = jnp.where(jnp.arange(NBOX, dtype=jnp.int32) == chosen, jnp.int32(NZ // 2), offsets)
    planes = jnp.arange(NLC, dtype=jnp.int32)
    groups = planes // NZ
    lower_box = jnp.maximum(groups - jax.random.randint(keys[1], (NLC,), 0, 2).astype(jnp.int32), 0)
    upper_box = jnp.minimum(lower_box + 1, NBOX - 1)
    lower_plane = (planes + offsets[lower_box]) % NZ
    upper_plane = (planes + offsets[upper_box]) % NZ
    lower_weight = jax.random.randint(keys[2], (NLC,), 0, WDEN + 1).astype(jnp.int32)
    return (lower_box, upper_box, lower_plane, upper_plane, lower_weight, WDEN - lower_weight)


def draw_box_lower(key, part):
    return routing(key)[0]


def draw_box_upper(key, part):
    return routing(key)[1]


def draw_plane_lower(key, part):
    return routing(key)[2]


def draw_plane_upper(key, part):
    return routing(key)[3]


def draw_weight_lower(key, part):
    return routing(key)[4]


def draw_weight_upper(key, part):
    return routing(key)[5]


def levels(stream_key, extent, pieces, smallest, top_value):
    level = 1.0
    for axis_at, blocks in pieces:
        heights = jax.random.uniform(jax.random.fold_in(jax.random.fold_in(stream_key, 6), axis_at), (blocks,), jnp.float32, smallest / len(pieces), top_value / len(pieces))
        level = level * jnp.repeat(jnp.exp(heights), extent[axis_at] // blocks).reshape((-1,) + (1,) * (len(extent) - 1 - axis_at))
    return level


def normal_values(rng, dims, width, bound, cuts=(), held_as=jnp.bfloat16):
    drawn = width * jax.random.normal(rng, dims, jnp.float32)
    if cuts:
        drawn = drawn * levels(rng, dims, cuts, -0.22, 0.18)
    return jnp.clip(drawn, -bound, bound).astype(held_as)


def setup_inputs(seed: int = 0) -> dict:
    arg_keys = jax.random.split(jax.random.key(seed), 10)
    hidden_field = normal_values(arg_keys[0], (NBOX, CH, NZ, NX, NY), 1.0, 6.0, ((0, 4), (2, 8)))
    cone_grad = normal_values(arg_keys[1], (NLC, NX, NY), 1.0, 6.0, ((0, 32),), jnp.float32)
    conv_weight = normal_values(arg_keys[2], (CH, 27), (CH * 27) ** -0.5, 0.4375)
    box_lower = draw_box_lower(jax.random.fold_in(arg_keys[9], 71), 0)
    box_upper = draw_box_upper(jax.random.fold_in(arg_keys[9], 71), 0)
    plane_lower = draw_plane_lower(jax.random.fold_in(arg_keys[9], 71), 0)
    plane_upper = draw_plane_upper(jax.random.fold_in(arg_keys[9], 71), 0)
    weight_lower = draw_weight_lower(jax.random.fold_in(arg_keys[9], 71), 0)
    weight_upper = draw_weight_upper(jax.random.fold_in(arg_keys[9], 71), 0)
    return {"hidden_field": hidden_field, "cone_grad": cone_grad, "conv_weight": conv_weight, "box_lower": box_lower, "box_upper": box_upper, "plane_lower": plane_lower, "plane_upper": plane_upper, "weight_lower": weight_lower, "weight_upper": weight_upper}


def tap_list():
    result = []
    for shift_z in (-1, 0, 1):
        for shift_x in (-1, 0, 1):
            for shift_y in (-1, 0, 1):
                result.append((shift_z, shift_x, shift_y))
    return result

def reference(hidden_field, cone_grad, conv_weight, box_lower, box_upper, plane_lower, plane_upper, weight_lower, weight_upper):
    lower = weight_lower.astype(jnp.float32) / WDEN
    upper = weight_upper.astype(jnp.float32) / WDEN
    first = jax.ops.segment_sum(lower[:, None, None] * cone_grad, (box_lower * NZ + plane_lower).astype(jnp.int32), num_segments=NBOX * NZ)
    second = jax.ops.segment_sum(upper[:, None, None] * cone_grad, (box_upper * NZ + plane_upper).astype(jnp.int32), num_segments=NBOX * NZ)
    field_grad = (first + second).reshape(NBOX, NZ, NX, NY)
    field_low = field_grad.astype(jnp.bfloat16)
    weight_wide = conv_weight.astype(jnp.float32)

    def per_box(pair):
        block, field = pair
        wide = block.astype(jnp.float32)
        grads = jnp.zeros((CH, NZ, NX, NY), jnp.float32)
        columns = []
        for index, shifts in enumerate(tap_list()):
            moved = jnp.roll(field, shifts, axis=(0, 1, 2)).astype(jnp.float32)
            grads = grads + weight_wide[:, index][:, None, None, None] * moved
            columns.append(lax.optimization_barrier(jnp.sum(wide * moved[None], axis=(1, 2, 3))))
        return (grads.astype(jnp.bfloat16), jnp.stack(columns, 1))
    hidden_grad, partial_value = lax.map(per_box, (hidden_field, field_low))
    weight_grad = lax.optimization_barrier(jnp.sum(partial_value, axis=0)) / jnp.sqrt(jnp.float32(NBOX * NZ * NX * NY))
    return (hidden_grad, weight_grad)
```

```python
import functools
import math

import jax
import jax.numpy as jnp
from jax import lax
from jax.experimental import pallas as pl
from jax.experimental.pallas import tpu as pltpu
from jax.sharding import PartitionSpec as P

WDEN = 256
MESH = pl.DeviceIdType.MESH
F32 = jnp.float32
BF16 = jnp.bfloat16
CHUNK = 32
EDGE = 8
NT = (((1,), (1,)), ((), ()))


def split(nx, nslab):
    rows = nx // nslab
    halves = 2 if rows % 16 == 0 else 1
    return halves, rows // halves


def kernel(nbox, nslab, scale, names, *refs):
    r = dict(zip(names, refs, strict=True))
    cone, weight, hbuf, out, wg = r["cone"], r["weight"], r["hbuf"], r["out"], r["wg"]
    bl, bu, plo, pup, wl, wu = (r[n] for n in ("bl", "bu", "plo", "pup", "wl", "wu"))
    own, z_up, z_dn = r["own"], r["z_up"], r["z_dn"]
    from_above, from_below = r["from_above"], r["from_below"]
    ht, wide, wmat, lmat, ft = r["ht"], r["wide"], r["wmat"], r["lmat"], r["ft"]
    msg, slab_terms, msg2, box_terms = r["msg"], r["slab_terms"], r["msg2"], r["box_terms"]

    g = lax.axis_index("box")
    me = lax.axis_index("slab")
    depth, nx, ny = cone.shape
    halves, rows = split(nx, nslab)
    part = nx // halves
    nz = depth * nslab
    ch = hbuf.shape[0]
    pairs = ch // 2
    chunks = ny // CHUNK
    window = CHUNK + 2 * EDGE
    send_a = [r["send_a%d" % h] for h in range(halves)]
    recv_a = [r["recv_a%d" % h] for h in range(halves)]
    send_b = [r["send_b%d" % h] for h in range(halves)]
    recv_b = [r["recv_b%d" % h] for h in range(halves)]

    smalls = [
        pltpu.make_async_copy(r[n + "_hbm"], r[n], r["isem"].at[i])
        for i, n in enumerate(("bl", "bu", "wl", "wu", "plo", "pup", "weight"))
    ]
    planes = [
        pltpu.make_async_copy(
            r["cone_hbm"].at[:, h * part : (h + 1) * part],
            cone.at[:, h * part : (h + 1) * part],
            r["csem"].at[h],
        )
        for h in range(halves)
    ]
    h_copy = pltpu.make_async_copy(r["h_hbm"], hbuf, r["hsem"].at[0])
    planes[0].start()
    for load in smalls:
        load.start()
    for load in planes[1:]:
        load.start()
    h_copy.start()

    barrier = pltpu.get_barrier_semaphore()

    def greet_slab(j, _):
        pl.semaphore_signal(barrier, inc=1, device_id={"slab": lax.rem(me + j, nslab)}, device_id_type=MESH)
        return 0

    def greet_box(j, _):
        pl.semaphore_signal(barrier, inc=1, device_id={"box": lax.rem(g + j, nbox)}, device_id_type=MESH)
        return 0

    lax.fori_loop(1, nslab, greet_slab, 0)
    lax.fori_loop(1, nbox, greet_box, 0)

    def weigh(h):
        def one(i, _):
            lower = wl[i].astype(F32) * (1.0 / WDEN)
            upper = wu[i].astype(F32) * (1.0 / WDEN)
            own_c = jnp.where(bl[i] == g, lower, 0.0) + jnp.where(bu[i] == g, upper, 0.0)
            below_c = jnp.where(bl[i] == g - 1, lower, 0.0)
            above_c = jnp.where(bu[i] == g + 1, upper, 0.0)
            plane = cone[i, h * part : (h + 1) * part].reshape(nslab, rows, ny)
            z_up[h, :, i] = (above_c * plane).astype(BF16)
            z_dn[h, :, i] = (below_c * plane).astype(BF16)
            own[h, :, i] = own_c * plane
            return 0

        lax.fori_loop(0, depth, one, 0)

    def up_copy(h, t):
        return pltpu.make_async_remote_copy(
            src_ref=z_up.at[h, t],
            dst_ref=from_below.at[h, t],
            send_sem=r["up_s"].at[h, t],
            recv_sem=r["up_r"].at[h, t],
            device_id={"box": lax.rem(g + 1, nbox)},
            device_id_type=MESH,
        )

    def dn_copy(h, t):
        return pltpu.make_async_remote_copy(
            src_ref=z_dn.at[h, t],
            dst_ref=from_above.at[h, t],
            send_sem=r["dn_s"].at[h, t],
            recv_sem=r["dn_r"].at[h, t],
            device_id={"box": lax.rem(g + nbox - 1, nbox)},
            device_id_type=MESH,
        )

    def send_z(h):
        def one(j, _):
            t = lax.rem(me + 1 + j, nslab)

            @pl.when(g < nbox - 1)
            def _():
                up_copy(h, t).start()

            @pl.when(g > 0)
            def _():
                dn_copy(h, t).start()

            return 0

        lax.fori_loop(0, nslab, one, 0)

    def a_copy(h, t, source):
        return pltpu.make_async_remote_copy(
            src_ref=send_a[h].at[t],
            dst_ref=recv_a[h].at[pl.ds(source * depth, depth)],
            send_sem=r["a_s"].at[h, t],
            recv_sem=r["a_r"].at[h, source],
            device_id={"slab": t},
            device_id_type=MESH,
        )

    def merge(h, t):
        @pl.when(g < nbox - 1)
        def _():
            dn_copy(h, t).wait_recv()
            own[h, t] = own[h, t] + from_above[h, t].astype(F32)

        @pl.when(g > 0)
        def _():
            up_copy(h, t).wait_recv()
            own[h, t] = own[h, t] + from_below[h, t].astype(F32)

    def merge_send(h, first, last, beside=None):
        def one(j, _):
            t = lax.rem(me + 1 + j, nslab)
            merge(h, t)
            send_a[h][t] = own[h, t].astype(BF16)
            a_copy(h, t, me).start()
            if beside is not None:
                beside(j)
            return 0

        lax.fori_loop(first, min(last, nslab - 1), one, 0)
        if last == nslab:
            merge(h, me)
            recv_a[h][pl.ds(me * depth, depth)] = own[h, me].astype(BF16)

    def wait_a(h):
        def one(j, _):
            source = lax.rem(me + j, nslab)
            a_copy(h, source, source).wait_recv()
            return 0

        lax.fori_loop(1, nslab, one, 0)

    def b_copy(h, s, source):
        return pltpu.make_async_remote_copy(
            src_ref=send_b[h].at[s],
            dst_ref=recv_b[h].at[source],
            send_sem=r["b_s"].at[h, s],
            recv_sem=r["b_r"].at[h, source],
            device_id={"slab": s},
            device_id_type=MESH,
        )

    def turn_send(h):
        offset = jnp.where(bl[0] == g, plo[0], pup[0]) - me * depth

        def wanted(s, q):
            return recv_a[h][lax.rem(s * depth - 1 + q - offset + 2 * nz, nz)]

        def one(j, _):
            s = lax.rem(me + 1 + j, nslab)
            for q in range(depth + 2):
                send_b[h][s, q] = wanted(s, q)
            b_copy(h, s, me).start()
            return 0

        lax.fori_loop(0, nslab - 1, one, 0)
        for q in range(depth + 2):
            recv_b[h][me, q] = wanted(me, q)

    def wait_b(h):
        def one(j, _):
            source = lax.rem(me + j, nslab)
            b_copy(h, source, source).wait_recv()
            return 0

        lax.fori_loop(1, nslab, one, 0)

    def turn(c):
        for z in range(depth):
            turned = hbuf[c, z].T
            for q in range(chunks):
                ht[q, pl.ds(pl.multiple_of(c * CHUNK, CHUNK), CHUNK), z * nx : (z + 1) * nx] = turned[
                    q * CHUNK : (q + 1) * CHUNK
                ]

    def turn_beside(j):
        @pl.when(j < ch)
        def _():
            turn(j)

    def fill_taps():
        y_in = lax.broadcasted_iota(jnp.int32, (ny, ny), 0)
        y_out = lax.broadcasted_iota(jnp.int32, (ny, ny), 1)
        hits = [y_in == lax.rem(y_out - dy + ny, ny) for dy in (-1, 0, 1)]
        taps = weight[...].astype(F32)
        for k in range(27):
            wide[k] = jnp.broadcast_to(taps[:, k : k + 1], (ch, ny))

        def one(p, _):
            for cc in range(2):
                for j in range(9):
                    block = jnp.zeros((ny, ny), F32)
                    for d in range(3):
                        block = jnp.where(hits[d], wide[3 * j + d, pl.ds(2 * p + cc, 1)], block)
                    wmat[p, j * ny : (j + 1) * ny, cc * ny : (cc + 1) * ny] = block.astype(BF16)
            return 0

        lax.fori_loop(0, pairs, one, 0)

    for load in smalls:
        load.wait()
    planes[0].wait()
    weigh(0)
    pl.semaphore_wait(barrier, nslab - 1 + nbox - 1)
    send_z(0)
    for h in range(1, halves):
        planes[h].wait()
        weigh(h)
        send_z(h)

    fill_taps()
    h_copy.wait()
    merge_send(0, 0, nslab, turn_beside)
    for c in range(nslab - 1, ch):
        turn(c)
    for h in range(1, halves):
        merge_send(h, 0, nslab // 2)
        wait_a(h - 1)
        turn_send(h - 1)
        merge_send(h, nslab // 2, nslab)
    wait_a(halves - 1)
    turn_send(halves - 1)
    for h in range(halves):
        wait_b(h)

    for q in range(depth + 2):
        plane = jnp.concatenate([recv_b[h][:, q].astype(F32).reshape(part, ny) for h in range(halves)], axis=0)
        for dx in (-1, 0, 1):
            moved = (plane if dx == 0 else pltpu.roll(plane, dx % nx, 0)).astype(BF16)
            for dz in (-1, 0, 1):
                z, j = q + dz - 1, (dz + 1) * 3 + dx + 1
                if 0 <= z < depth:
                    lmat[z * nx : (z + 1) * nx, j * ny : (j + 1) * ny] = moved
            turned = moved.T
            at = slice(q * nx, (q + 1) * nx)
            ft[dx + 1, EDGE : EDGE + ny, at] = turned
            ft[dx + 1, 0:EDGE, at] = turned[ny - EDGE : ny]
            ft[dx + 1, EDGE + ny : EDGE + ny + EDGE, at] = turned[0:EDGE]

    product = None
    for q in range(chunks):
        field = jnp.concatenate(
            [
                ft[dx + 1, q * CHUNK : q * CHUNK + window, (1 - dz) * nx : (1 - dz + depth) * nx]
                for dz in (-1, 0, 1)
                for dx in (-1, 0, 1)
            ],
            axis=0,
        )
        term = lax.dot_general(field, ht[q], NT, preferred_element_type=F32)
        product = term if product is None else product + term
    product = product.reshape(9, window, ch * CHUNK)
    w_row = lax.broadcasted_iota(jnp.int32, (window, ch * CHUNK), 0)
    w_y = lax.rem(lax.broadcasted_iota(jnp.int32, (window, ch * CHUNK), 1), CHUNK)
    picks = [w_row == w_y + EDGE - dy for dy in (-1, 0, 1)]
    sums = [
        jnp.sum(jnp.where(picks[d], product[j], 0.0), axis=0, keepdims=True) for j in range(9) for d in range(3)
    ]
    sums.append(jnp.zeros((5, ch * CHUNK), F32))
    by_tap = jnp.concatenate(sums, axis=0)
    msg[...] = jnp.zeros_like(msg)
    msg[:, 0:32] = jnp.sum(by_tap.T.reshape(ch, CHUNK, 32), axis=1)

    def c_copy(s, source):
        return pltpu.make_async_remote_copy(
            src_ref=msg,
            dst_ref=slab_terms.at[source],
            send_sem=r["c_s"].at[s],
            recv_sem=r["c_r"].at[source],
            device_id={"slab": s},
            device_id_type=MESH,
        )

    def d_copy(b, source):
        return pltpu.make_async_remote_copy(
            src_ref=msg2,
            dst_ref=box_terms.at[source],
            send_sem=r["d_s"].at[b],
            recv_sem=r["d_r"].at[source],
            device_id={"box": b},
            device_id_type=MESH,
        )

    def send_c(j, _):
        c_copy(lax.rem(me + j, nslab), me).start()
        return 0

    def send_d(j, _):
        d_copy(lax.rem(g + j, nbox), g).start()
        return 0

    def wait_c(j, _):
        source = lax.rem(me + j, nslab)
        c_copy(source, source).wait_recv()
        return 0

    def wait_d(j, _):
        source = lax.rem(g + j, nbox)
        d_copy(source, source).wait_recv()
        return 0

    def pair_grads(p, _):
        grads = jnp.dot(lmat[...], wmat[p], preferred_element_type=F32)
        for cc in range(2):
            out[2 * p + cc] = grads[:, cc * ny : (cc + 1) * ny].reshape(depth, nx, ny).astype(BF16)
        return 0

    slab_terms[me] = msg[...]
    lax.fori_loop(1, nslab, send_c, 0)
    lax.fori_loop(0, pairs // 2, pair_grads, 0)
    lax.fori_loop(1, nslab, wait_c, 0)
    total = slab_terms[0]
    for s in range(1, nslab):
        total = total + slab_terms[s]
    msg2[...] = total
    box_terms[g] = total
    lax.fori_loop(1, nbox, send_d, 0)
    lax.fori_loop(pairs // 2, pairs, pair_grads, 0)
    lax.fori_loop(1, nbox, wait_d, 0)
    total = box_terms[0]
    for b in range(1, nbox):
        total = total + box_terms[b]
    wg[...] = (total * scale)[:, 0:27]

    def drain_z(t, _):
        for h in range(halves):

            @pl.when(g < nbox - 1)
            def _():
                up_copy(h, t).wait_send()

            @pl.when(g > 0)
            def _():
                dn_copy(h, t).wait_send()

        return 0

    def drain_slab(j, _):
        s = lax.rem(me + j, nslab)
        for h in range(halves):
            a_copy(h, s, me).wait_send()
            b_copy(h, s, me).wait_send()
        c_copy(s, me).wait_send()
        return 0

    def drain_box(j, _):
        d_copy(lax.rem(g + j, nbox), g).wait_send()
        return 0

    lax.fori_loop(0, nslab, drain_z, 0)
    lax.fori_loop(1, nslab, drain_slab, 0)
    lax.fori_loop(1, nbox, drain_box, 0)


def local(
    nbox,
    nslab,
    hidden_field,
    cone_grad,
    conv_weight,
    box_lower,
    box_upper,
    plane_lower,
    plane_upper,
    weight_lower,
    weight_upper,
):
    _, ch, depth, nx, ny = hidden_field.shape
    halves, rows = split(nx, nslab)
    nz = depth * nslab
    scale = 1.0 / math.sqrt(nbox * nz * nx * ny)
    vmem = pl.BlockSpec(memory_space=pltpu.VMEM)
    hbm = pl.BlockSpec(memory_space=pltpu.HBM)
    dma = pltpu.SemaphoreType.DMA
    ins = {
        "bl_hbm": box_lower,
        "bu_hbm": box_upper,
        "plo_hbm": plane_lower,
        "pup_hbm": plane_upper,
        "wl_hbm": weight_lower,
        "wu_hbm": weight_upper,
        "cone_hbm": cone_grad,
        "weight_hbm": conv_weight,
        "h_hbm": hidden_field.reshape(ch, depth, nx, ny),
    }
    chunk = (halves, nslab, depth, rows, ny)
    scratch = {n: pltpu.SMEM((depth,), jnp.int32) for n in ("bl", "bu", "plo", "pup", "wl", "wu")}
    scratch["cone"] = pltpu.VMEM(cone_grad.shape, F32)
    scratch["weight"] = pltpu.VMEM(conv_weight.shape, BF16)
    scratch["hbuf"] = pltpu.VMEM((ch, depth, nx, ny), BF16)
    scratch["own"] = pltpu.VMEM(chunk, F32)
    for n in ("z_up", "z_dn", "from_above", "from_below"):
        scratch[n] = pltpu.VMEM(chunk, BF16)
    for h in range(halves):
        scratch["send_a%d" % h] = pltpu.VMEM(chunk[1:], BF16)
        scratch["recv_a%d" % h] = pltpu.VMEM((nz, rows, ny), BF16)
        scratch["send_b%d" % h] = pltpu.VMEM((nslab, depth + 2, rows, ny), BF16)
        scratch["recv_b%d" % h] = pltpu.VMEM((nslab, depth + 2, rows, ny), BF16)
    scratch["ht"] = pltpu.VMEM((ny // CHUNK, ch * CHUNK, depth * nx), BF16)
    scratch["wide"] = pltpu.VMEM((27, ch, ny), F32)
    scratch["wmat"] = pltpu.VMEM((ch // 2, 9 * ny, 2 * ny), BF16)
    scratch["lmat"] = pltpu.VMEM((depth * nx, 9 * ny), BF16)
    scratch["ft"] = pltpu.VMEM((3, ny + 2 * EDGE, (depth + 2) * nx), BF16)
    scratch["msg"] = pltpu.VMEM((ch, 128), F32)
    scratch["slab_terms"] = pltpu.VMEM((nslab, ch, 128), F32)
    scratch["msg2"] = pltpu.VMEM((ch, 128), F32)
    scratch["box_terms"] = pltpu.VMEM((nbox, ch, 128), F32)
    scratch["isem"] = dma((7,))
    scratch["csem"] = dma((halves,))
    scratch["hsem"] = dma((1,))
    for n in ("up", "dn", "a", "b"):
        scratch[n + "_s"] = dma((halves, nslab))
        scratch[n + "_r"] = dma((halves, nslab))
    scratch["c_s"] = dma((nslab,))
    scratch["c_r"] = dma((nslab,))
    scratch["d_s"] = dma((nbox,))
    scratch["d_r"] = dma((nbox,))
    names = (*ins, "out", "wg", *scratch)
    hidden_grad, weight_grad = pl.pallas_call(
        functools.partial(kernel, nbox, nslab, scale, names),
        out_shape=(
            pltpu.VMEM((ch, depth, nx, ny), BF16),
            jax.ShapeDtypeStruct((ch, 27), F32),
        ),
        in_specs=[hbm] * len(ins),
        out_specs=(vmem, vmem),
        scratch_shapes=list(scratch.values()),
        compiler_params=pltpu.CompilerParams(
            collective_id=0, has_side_effects=True, vmem_limit_bytes=int(44 * 2**20)
        ),
    )(*(pltpu.with_memory_space_constraint(x, pltpu.HBM) for x in ins.values()))
    return hidden_grad.reshape(hidden_field.shape), weight_grad


def solution(mesh):
    in_specs = (
        P("box", None, "slab", None, None),
        P(("box", "slab"), None, None),
        P(),
        P(("box", "slab")),
        P(("box", "slab")),
        P(("box", "slab")),
        P(("box", "slab")),
        P(("box", "slab")),
        P(("box", "slab")),
    )
    out_specs = (P("box", None, "slab", None, None), P())
    return jax.shard_map(
        functools.partial(local, mesh.shape["box"], mesh.shape["slab"]),
        mesh=mesh,
        in_specs=in_specs,
        out_specs=out_specs,
        check_vma=False,
    )
```

```python
import functools
import math

import jax
import jax.numpy as jnp
from jax import lax
from jax.experimental import pallas as pl
from jax.experimental.pallas import tpu as pltpu
from jax.sharding import PartitionSpec as P

WDEN = 256
MESH = pl.DeviceIdType.MESH
F32 = jnp.float32
BF16 = jnp.bfloat16
CHUNK = 32
EDGE = 8
NT = (((1,), (1,)), ((), ()))


def split(nx, nslab):
    rows = nx // nslab
    halves = 2 if rows % 16 == 0 else 1
    return halves, rows // halves


def kernel(nbox, nslab, scale, names, *refs):
    r = dict(zip(names, refs, strict=True))
    cone, weight, hbuf, out, wg = r["cone"], r["weight"], r["hbuf"], r["out"], r["wg"]
    bl, bu, plo, pup, wl, wu = (r[n] for n in ("bl", "bu", "plo", "pup", "wl", "wu"))
    own, z_up, z_dn = r["own"], r["z_up"], r["z_dn"]
    from_above, from_below = r["from_above"], r["from_below"]
    ht, wide, wmat, lmat, ft = r["ht"], r["wide"], r["wmat"], r["lmat"], r["ft"]
    msg, terms = r["msg"], r["terms"]

    g = lax.axis_index("box")
    me = lax.axis_index("slab")
    depth, nx, ny = cone.shape
    halves, rows = split(nx, nslab)
    part = nx // halves
    nz = depth * nslab
    ch = hbuf.shape[0]
    pairs = ch // 2
    chunks = ny // CHUNK
    window = CHUNK + 2 * EDGE
    send_a = [r["send_a%d" % h] for h in range(halves)]
    recv_a = [r["recv_a%d" % h] for h in range(halves)]
    send_b = [r["send_b%d" % h] for h in range(halves)]
    recv_b = [r["recv_b%d" % h] for h in range(halves)]

    smalls = [
        pltpu.make_async_copy(r[n + "_hbm"], r[n], r["isem"].at[i])
        for i, n in enumerate(("bl", "bu", "wl", "wu", "plo", "pup", "weight"))
    ]
    planes = [
        pltpu.make_async_copy(
            r["cone_hbm"].at[:, h * part : (h + 1) * part],
            cone.at[:, h * part : (h + 1) * part],
            r["csem"].at[h],
        )
        for h in range(halves)
    ]
    h_copy = pltpu.make_async_copy(r["h_hbm"], hbuf, r["hsem"].at[0])
    planes[0].start()
    for load in smalls:
        load.start()
    for load in planes[1:]:
        load.start()
    h_copy.start()

    barrier = pltpu.get_barrier_semaphore()

    def greet_slab(j, _):
        pl.semaphore_signal(barrier, inc=1, device_id={"slab": lax.rem(me + j, nslab)}, device_id_type=MESH)
        return 0

    def greet_box(j, _):
        pl.semaphore_signal(barrier, inc=1, device_id={"box": lax.rem(g + j, nbox)}, device_id_type=MESH)
        return 0

    lax.fori_loop(1, nslab, greet_slab, 0)
    lax.fori_loop(1, nbox, greet_box, 0)

    def weigh(h):
        def one(i, _):
            lower = wl[i].astype(F32) * (1.0 / WDEN)
            upper = wu[i].astype(F32) * (1.0 / WDEN)
            own_c = jnp.where(bl[i] == g, lower, 0.0) + jnp.where(bu[i] == g, upper, 0.0)
            below_c = jnp.where(bl[i] == g - 1, lower, 0.0)
            above_c = jnp.where(bu[i] == g + 1, upper, 0.0)
            plane = cone[i, h * part : (h + 1) * part].reshape(nslab, rows, ny)
            z_up[h, :, i] = (above_c * plane).astype(BF16)
            z_dn[h, :, i] = (below_c * plane).astype(BF16)
            own[h, :, i] = own_c * plane
            return 0

        lax.fori_loop(0, depth, one, 0)

    def up_copy(h, t):
        return pltpu.make_async_remote_copy(
            src_ref=z_up.at[h, t],
            dst_ref=from_below.at[h, t],
            send_sem=r["up_s"].at[h, t],
            recv_sem=r["up_r"].at[h, t],
            device_id={"box": lax.rem(g + 1, nbox)},
            device_id_type=MESH,
        )

    def dn_copy(h, t):
        return pltpu.make_async_remote_copy(
            src_ref=z_dn.at[h, t],
            dst_ref=from_above.at[h, t],
            send_sem=r["dn_s"].at[h, t],
            recv_sem=r["dn_r"].at[h, t],
            device_id={"box": lax.rem(g + nbox - 1, nbox)},
            device_id_type=MESH,
        )

    def send_z(h):
        def one(j, _):
            t = lax.rem(me + 1 + j, nslab)

            @pl.when(g < nbox - 1)
            def _():
                up_copy(h, t).start()

            @pl.when(g > 0)
            def _():
                dn_copy(h, t).start()

            return 0

        lax.fori_loop(0, nslab, one, 0)

    def a_copy(h, t, source):
        return pltpu.make_async_remote_copy(
            src_ref=send_a[h].at[t],
            dst_ref=recv_a[h].at[pl.ds(source * depth, depth)],
            send_sem=r["a_s"].at[h, t],
            recv_sem=r["a_r"].at[h, source],
            device_id={"slab": t},
            device_id_type=MESH,
        )

    def merge(h, t):
        @pl.when(g < nbox - 1)
        def _():
            dn_copy(h, t).wait_recv()
            own[h, t] = own[h, t] + from_above[h, t].astype(F32)

        @pl.when(g > 0)
        def _():
            up_copy(h, t).wait_recv()
            own[h, t] = own[h, t] + from_below[h, t].astype(F32)

    def merge_send(h, beside=None):
        def one(j, _):
            t = lax.rem(me + 1 + j, nslab)
            merge(h, t)
            send_a[h][t] = own[h, t].astype(BF16)
            a_copy(h, t, me).start()
            if beside is not None:
                beside(j)
            return 0

        lax.fori_loop(0, nslab - 1, one, 0)
        merge(h, me)
        recv_a[h][pl.ds(me * depth, depth)] = own[h, me].astype(BF16)

    def wait_a(h):
        def one(j, _):
            source = lax.rem(me + j, nslab)
            a_copy(h, source, source).wait_recv()
            return 0

        lax.fori_loop(1, nslab, one, 0)

    def b_copy(h, s, source):
        return pltpu.make_async_remote_copy(
            src_ref=send_b[h].at[s],
            dst_ref=recv_b[h].at[source],
            send_sem=r["b_s"].at[h, s],
            recv_sem=r["b_r"].at[h, source],
            device_id={"slab": s},
            device_id_type=MESH,
        )

    def turn_send(h):
        offset = jnp.where(bl[0] == g, plo[0], pup[0]) - me * depth

        def wanted(s):
            first = lax.rem(s * depth - 1 - offset + 2 * nz, nz)
            for q in range(depth + 2):
                at = first + q
                yield q, recv_a[h][jnp.where(at >= nz, at - nz, at)]

        def one(j, _):
            s = lax.rem(me + 1 + j, nslab)
            for q, plane in wanted(s):
                send_b[h][s, q] = plane
            b_copy(h, s, me).start()
            return 0

        lax.fori_loop(0, nslab - 1, one, 0)
        for q, plane in wanted(me):
            recv_b[h][me, q] = plane

    def wait_b(h):
        def one(j, _):
            source = lax.rem(me + j, nslab)
            b_copy(h, source, source).wait_recv()
            return 0

        lax.fori_loop(1, nslab, one, 0)

    def turn(c):
        for z in range(depth):
            turned = hbuf[c, z].T
            for q in range(chunks):
                ht[q, pl.ds(pl.multiple_of(c * CHUNK, CHUNK), CHUNK), z * nx : (z + 1) * nx] = turned[
                    q * CHUNK : (q + 1) * CHUNK
                ]

    def turn_beside(j):
        @pl.when(j < ch)
        def _():
            turn(j)

    def fill_taps():
        y_in = lax.broadcasted_iota(jnp.int32, (ny, ny), 0)
        y_out = lax.broadcasted_iota(jnp.int32, (ny, ny), 1)
        hits = [y_in == lax.rem(y_out - dy + ny, ny) for dy in (-1, 0, 1)]
        taps = weight[...].astype(F32)
        for k in range(27):
            wide[k] = jnp.broadcast_to(taps[:, k : k + 1], (ch, ny))

        def one(p, _):
            for cc in range(2):
                for j in range(9):
                    block = jnp.zeros((ny, ny), F32)
                    for d in range(3):
                        block = jnp.where(hits[d], wide[3 * j + d, pl.ds(2 * p + cc, 1)], block)
                    wmat[p, j * ny : (j + 1) * ny, cc * ny : (cc + 1) * ny] = block.astype(BF16)
            return 0

        lax.fori_loop(0, pairs, one, 0)

    for load in smalls:
        load.wait()
    planes[0].wait()
    weigh(0)
    pl.semaphore_wait(barrier, nslab - 1 + nbox - 1)
    send_z(0)
    for h in range(1, halves):
        planes[h].wait()
        weigh(h)
        send_z(h)

    fill_taps()
    h_copy.wait()
    merge_send(0, turn_beside)
    for c in range(nslab - 1, ch):
        turn(c)
    for h in range(1, halves):
        merge_send(h)
        wait_a(h - 1)
        turn_send(h - 1)
    wait_a(halves - 1)
    turn_send(halves - 1)
    for h in range(halves):
        wait_b(h)

    for q in range(depth + 2):
        plane = jnp.concatenate([recv_b[h][:, q].astype(F32).reshape(part, ny) for h in range(halves)], axis=0)
        for dx in (-1, 0, 1):
            moved = (plane if dx == 0 else pltpu.roll(plane, dx % nx, 0)).astype(BF16)
            for dz in (-1, 0, 1):
                z, j = q + dz - 1, (dz + 1) * 3 + dx + 1
                if 0 <= z < depth:
                    lmat[z * nx : (z + 1) * nx, j * ny : (j + 1) * ny] = moved
            turned = moved.T
            at = slice(q * nx, (q + 1) * nx)
            ft[dx + 1, EDGE : EDGE + ny, at] = turned
            ft[dx + 1, 0:EDGE, at] = turned[ny - EDGE : ny]
            ft[dx + 1, EDGE + ny : EDGE + ny + EDGE, at] = turned[0:EDGE]

    product = None
    for q in range(chunks):
        field = jnp.concatenate(
            [
                ft[dx + 1, q * CHUNK : q * CHUNK + window, (1 - dz) * nx : (1 - dz + depth) * nx]
                for dz in (-1, 0, 1)
                for dx in (-1, 0, 1)
            ],
            axis=0,
        )
        term = lax.dot_general(field, ht[q], NT, preferred_element_type=F32)
        product = term if product is None else product + term
    product = product.reshape(9, window, ch * CHUNK)
    w_row = lax.broadcasted_iota(jnp.int32, (window, ch * CHUNK), 0)
    w_y = lax.rem(lax.broadcasted_iota(jnp.int32, (window, ch * CHUNK), 1), CHUNK)
    picks = [w_row == w_y + EDGE - dy for dy in (-1, 0, 1)]
    sums = [
        jnp.sum(jnp.where(picks[d], product[j], 0.0), axis=0, keepdims=True) for j in range(9) for d in range(3)
    ]
    sums.append(jnp.zeros((5, ch * CHUNK), F32))
    by_tap = jnp.concatenate(sums, axis=0)
    by_channel = jnp.sum(by_tap.T.reshape(ch, CHUNK, 32), axis=1)
    by_channel = jnp.concatenate([by_channel, jnp.zeros((ch, 96), F32)], axis=1)
    of_four = lax.rem(lax.broadcasted_iota(jnp.int32, (ch, 128), 0), 4)
    packed = jnp.where(of_four == 0, by_channel, 0.0)
    for i in range(1, 4):
        packed = packed + pltpu.roll(jnp.where(of_four == i, by_channel, 0.0), 32 * i, 1)
    packed = jnp.sum(packed.reshape(ch // 4, 4, 128), axis=1)
    ndev = nbox * nslab
    my = g * nslab + me
    msg[...] = packed
    terms[my] = packed

    def r_copy(to, source):
        return pltpu.make_async_remote_copy(
            src_ref=msg,
            dst_ref=terms.at[source],
            send_sem=r["r_s"].at[to],
            recv_sem=r["r_r"].at[source],
            device_id={"box": to // nslab, "slab": lax.rem(to, nslab)},
            device_id_type=MESH,
        )

    def send_r(j, _):
        r_copy(lax.rem(my + j, ndev), my).start()
        return 0

    def wait_r(j, _):
        source = lax.rem(my + j, ndev)
        r_copy(source, source).wait_recv()
        return 0

    def pair_grads(p, _):
        grads = jnp.dot(lmat[...], wmat[p], preferred_element_type=F32)
        for cc in range(2):
            out[2 * p + cc] = grads[:, cc * ny : (cc + 1) * ny].reshape(depth, nx, ny).astype(BF16)
        return 0

    lax.fori_loop(1, ndev, send_r, 0)
    lax.fori_loop(0, pairs, pair_grads, 0)

    def drain_z(t, _):
        for h in range(halves):

            @pl.when(g < nbox - 1)
            def _():
                up_copy(h, t).wait_send()

            @pl.when(g > 0)
            def _():
                dn_copy(h, t).wait_send()

        return 0

    def drain_slab(j, _):
        s = lax.rem(me + j, nslab)
        for h in range(halves):
            a_copy(h, s, me).wait_send()
            b_copy(h, s, me).wait_send()
        return 0

    def drain_r(j, _):
        r_copy(lax.rem(my + j, ndev), my).wait_send()
        return 0

    lax.fori_loop(0, nslab, drain_z, 0)
    lax.fori_loop(1, nslab, drain_slab, 0)
    lax.fori_loop(1, ndev, drain_r, 0)
    lax.fori_loop(1, ndev, wait_r, 0)
    total = jnp.sum(terms[...], axis=0) * scale
    for c in range(ch):
        wg[c : c + 1, :] = total[c // 4 : c // 4 + 1, (c % 4) * 32 : (c % 4) * 32 + 27]


def write(grads, terms, out, wg, sem):
    copies = [pltpu.make_async_copy(terms, wg, sem.at[0])]
    copies += [pltpu.make_async_copy(grads.at[c], out.at[c], sem.at[c + 1]) for c in range(grads.shape[0])]
    for copy in copies:
        copy.start()
    for copy in copies:
        copy.wait()


def local(
    nbox,
    nslab,
    hidden_field,
    cone_grad,
    conv_weight,
    box_lower,
    box_upper,
    plane_lower,
    plane_upper,
    weight_lower,
    weight_upper,
):
    _, ch, depth, nx, ny = hidden_field.shape
    halves, rows = split(nx, nslab)
    nz = depth * nslab
    scale = 1.0 / math.sqrt(nbox * nz * nx * ny)
    vmem = pl.BlockSpec(memory_space=pltpu.VMEM)
    hbm = pl.BlockSpec(memory_space=pltpu.HBM)
    dma = pltpu.SemaphoreType.DMA
    ins = {
        "bl_hbm": box_lower,
        "bu_hbm": box_upper,
        "plo_hbm": plane_lower,
        "pup_hbm": plane_upper,
        "wl_hbm": weight_lower,
        "wu_hbm": weight_upper,
        "cone_hbm": cone_grad,
        "weight_hbm": conv_weight,
        "h_hbm": hidden_field.reshape(ch, depth, nx, ny),
    }
    chunk = (halves, nslab, depth, rows, ny)
    scratch = {n: pltpu.SMEM((depth,), jnp.int32) for n in ("bl", "bu", "plo", "pup", "wl", "wu")}
    scratch["cone"] = pltpu.VMEM(cone_grad.shape, F32)
    scratch["weight"] = pltpu.VMEM(conv_weight.shape, BF16)
    scratch["hbuf"] = pltpu.VMEM((ch, depth, nx, ny), BF16)
    scratch["own"] = pltpu.VMEM(chunk, F32)
    for n in ("z_up", "z_dn", "from_above", "from_below"):
        scratch[n] = pltpu.VMEM(chunk, BF16)
    for h in range(halves):
        scratch["send_a%d" % h] = pltpu.VMEM(chunk[1:], BF16)
        scratch["recv_a%d" % h] = pltpu.VMEM((nz, rows, ny), BF16)
        scratch["send_b%d" % h] = pltpu.VMEM((nslab, depth + 2, rows, ny), BF16)
        scratch["recv_b%d" % h] = pltpu.VMEM((nslab, depth + 2, rows, ny), BF16)
    scratch["ht"] = pltpu.VMEM((ny // CHUNK, ch * CHUNK, depth * nx), BF16)
    scratch["wide"] = pltpu.VMEM((27, ch, ny), F32)
    scratch["wmat"] = pltpu.VMEM((ch // 2, 9 * ny, 2 * ny), BF16)
    scratch["lmat"] = pltpu.VMEM((depth * nx, 9 * ny), BF16)
    scratch["ft"] = pltpu.VMEM((3, ny + 2 * EDGE, (depth + 2) * nx), BF16)
    scratch["msg"] = pltpu.VMEM((ch // 4, 128), F32)
    scratch["terms"] = pltpu.VMEM((nbox * nslab, ch // 4, 128), F32)
    scratch["isem"] = dma((7,))
    scratch["csem"] = dma((halves,))
    scratch["hsem"] = dma((1,))
    for n in ("up", "dn", "a", "b"):
        scratch[n + "_s"] = dma((halves, nslab))
        scratch[n + "_r"] = dma((halves, nslab))
    scratch["r_s"] = dma((nbox * nslab,))
    scratch["r_r"] = dma((nbox * nslab,))
    names = (*ins, "out", "wg", *scratch)
    hidden_grad, weight_grad = pl.pallas_call(
        functools.partial(kernel, nbox, nslab, scale, names),
        out_shape=(
            pltpu.VMEM((ch, depth, nx, ny), BF16),
            pltpu.VMEM((ch, 27), F32),
        ),
        in_specs=[hbm] * len(ins),
        out_specs=(vmem, vmem),
        scratch_shapes=list(scratch.values()),
        compiler_params=pltpu.CompilerParams(
            collective_id=0, has_side_effects=True, vmem_limit_bytes=int(44 * 2**20)
        ),
    )(*(pltpu.with_memory_space_constraint(x, pltpu.HBM) for x in ins.values()))
    hidden_grad, weight_grad = pl.pallas_call(
        write,
        out_shape=(pltpu.HBM(hidden_grad.shape, BF16), pltpu.HBM(weight_grad.shape, F32)),
        in_specs=[vmem, vmem],
        out_specs=(hbm, hbm),
        scratch_shapes=[dma((ch + 1,))],
    )(pltpu.with_memory_space_constraint(hidden_grad, pltpu.VMEM), pltpu.with_memory_space_constraint(weight_grad, pltpu.VMEM))
    return hidden_grad.reshape(hidden_field.shape), weight_grad


def solution(mesh):
    in_specs = (
        P("box", None, "slab", None, None),
        P(("box", "slab"), None, None),
        P(),
        P(("box", "slab")),
        P(("box", "slab")),
        P(("box", "slab")),
        P(("box", "slab")),
        P(("box", "slab")),
        P(("box", "slab")),
    )
    out_specs = (P("box", None, "slab", None, None), P())
    return jax.shard_map(
        functools.partial(local, mesh.shape["box"], mesh.shape["slab"]),
        mesh=mesh,
        in_specs=in_specs,
        out_specs=out_specs,
        check_vma=False,
    )
```

```python
import functools
import math

import jax
import jax.numpy as jnp
from jax import lax
from jax.experimental import pallas as pl
from jax.experimental.pallas import tpu as pltpu
from jax.sharding import PartitionSpec as P

WDEN = 256
MESH = pl.DeviceIdType.MESH
F32 = jnp.float32
BF16 = jnp.bfloat16
CHUNK = 32
EDGE = 8
NT = (((1,), (1,)), ((), ()))


def split(nx, nslab):
    rows = nx // nslab
    halves = 2 if rows % 16 == 0 else 1
    return halves, rows // halves


def other(at, j, size):
    bit, partner = 1, at
    while bit < size:
        if j & bit:
            partner = partner + bit * (1 - 2 * lax.rem(lax.div(at, bit), 2))
        bit *= 2
    return partner


def kernel(nbox, nslab, scale, names, *refs):
    r = dict(zip(names, refs, strict=True))
    cone, weight, hbuf, out, wg = r["cone"], r["weight"], r["hbuf"], r["out"], r["wg"]
    bl, bu, plo, pup, wl, wu = (r[n] for n in ("bl", "bu", "plo", "pup", "wl", "wu"))
    own, z_up, z_dn = r["own"], r["z_up"], r["z_dn"]
    from_above, from_below = r["from_above"], r["from_below"]
    ht, wide, wmat, lmat, ft = r["ht"], r["wide"], r["wmat"], r["lmat"], r["ft"]
    msg, terms = r["msg"], r["terms"]

    g = lax.axis_index("box")
    me = lax.axis_index("slab")
    depth, nx, ny = cone.shape
    halves, rows = split(nx, nslab)
    part = nx // halves
    nz = depth * nslab
    ch = hbuf.shape[0]
    pairs = ch // 2
    chunks = ny // CHUNK
    window = CHUNK + 2 * EDGE
    send_a = [r["send_a%d" % h] for h in range(halves)]
    recv_a = [r["recv_a%d" % h] for h in range(halves)]
    send_b = [r["send_b%d" % h] for h in range(halves)]
    recv_b = [r["recv_b%d" % h] for h in range(halves)]

    smalls = [
        pltpu.make_async_copy(r[n + "_hbm"], r[n], r["isem"].at[i])
        for i, n in enumerate(("bl", "bu", "wl", "wu", "plo", "pup", "weight"))
    ]
    planes = [
        pltpu.make_async_copy(
            r["cone_hbm"].at[:, h * part : (h + 1) * part],
            cone.at[:, h * part : (h + 1) * part],
            r["csem"].at[h],
        )
        for h in range(halves)
    ]
    h_copy = pltpu.make_async_copy(r["h_hbm"], hbuf, r["hsem"].at[0])
    planes[0].start()
    for load in smalls:
        load.start()
    for load in planes[1:]:
        load.start()
    h_copy.start()

    barrier = pltpu.get_barrier_semaphore()

    def greet_slab(j, _):
        pl.semaphore_signal(barrier, inc=1, device_id={"slab": lax.rem(me + j, nslab)}, device_id_type=MESH)
        return 0

    def greet_box(j, _):
        pl.semaphore_signal(barrier, inc=1, device_id={"box": lax.rem(g + j, nbox)}, device_id_type=MESH)
        return 0

    lax.fori_loop(1, nslab, greet_slab, 0)
    lax.fori_loop(1, nbox, greet_box, 0)

    def weigh(h):
        def one(i, _):
            lower = wl[i].astype(F32) * (1.0 / WDEN)
            upper = wu[i].astype(F32) * (1.0 / WDEN)
            own_c = jnp.where(bl[i] == g, lower, 0.0) + jnp.where(bu[i] == g, upper, 0.0)
            below_c = jnp.where(bl[i] == g - 1, lower, 0.0)
            above_c = jnp.where(bu[i] == g + 1, upper, 0.0)
            plane = cone[i, h * part : (h + 1) * part].reshape(nslab, rows, ny)
            z_up[h, :, i] = (above_c * plane).astype(BF16)
            z_dn[h, :, i] = (below_c * plane).astype(BF16)
            own[h, :, i] = own_c * plane
            return 0

        lax.fori_loop(0, depth, one, 0)

    def every(source, target, send, recv, at):
        return pltpu.make_async_remote_copy(
            src_ref=source,
            dst_ref=target,
            send_sem=send.at[at],
            recv_sem=recv.at[at],
            device_id={"slab": me},
            device_id_type=MESH,
        )

    def up_copy(h, t):
        return pltpu.make_async_remote_copy(
            src_ref=z_up.at[h, t],
            dst_ref=from_below.at[h, t],
            send_sem=r["up_s"].at[0],
            recv_sem=r["up_r"].at[h, t],
            device_id={"box": lax.rem(g + 1, nbox)},
            device_id_type=MESH,
        )

    def dn_copy(h, t):
        return pltpu.make_async_remote_copy(
            src_ref=z_dn.at[h, t],
            dst_ref=from_above.at[h, t],
            send_sem=r["dn_s"].at[0],
            recv_sem=r["dn_r"].at[h, t],
            device_id={"box": lax.rem(g + nbox - 1, nbox)},
            device_id_type=MESH,
        )

    def send_z(h):
        for j in reversed(range(nslab)):
            t = other(me, j, nslab)

            @pl.when(g < nbox - 1)
            def _():
                up_copy(h, t).start()

            @pl.when(g > 0)
            def _():
                dn_copy(h, t).start()

    def a_copy(h, t, source):
        return pltpu.make_async_remote_copy(
            src_ref=send_a[h].at[t],
            dst_ref=recv_a[h].at[pl.ds(source * depth, depth)],
            send_sem=r["a_s"].at[h],
            recv_sem=r["a_r"].at[h],
            device_id={"slab": t},
            device_id_type=MESH,
        )

    def merge(h, t):
        @pl.when(g < nbox - 1)
        def _():
            dn_copy(h, t).wait_recv()
            own[h, t] = own[h, t] + from_above[h, t].astype(F32)

        @pl.when(g > 0)
        def _():
            up_copy(h, t).wait_recv()
            own[h, t] = own[h, t] + from_below[h, t].astype(F32)

    def merge_send(h, beside=None):
        for j in reversed(range(1, nslab)):
            t = other(me, j, nslab)
            merge(h, t)
            send_a[h][t] = own[h, t].astype(BF16)
            a_copy(h, t, me).start()
            if beside is not None:
                beside(nslab - 1 - j)
        merge(h, me)
        recv_a[h][pl.ds(me * depth, depth)] = own[h, me].astype(BF16)

    def wait_a(h):
        every(send_a[h].at[: nslab - 1], recv_a[h].at[: (nslab - 1) * depth], r["a_s"], r["a_r"], h).wait_recv()

    def b_copy(h, s, source):
        return pltpu.make_async_remote_copy(
            src_ref=send_b[h].at[s],
            dst_ref=recv_b[h].at[source],
            send_sem=r["b_s"].at[h],
            recv_sem=r["b_r"].at[h],
            device_id={"slab": s},
            device_id_type=MESH,
        )

    def turn_send(h):
        offset = jnp.where(bl[0] == g, plo[0], pup[0]) - me * depth

        def wanted(s):
            first = lax.rem(s * depth - 1 - offset + 2 * nz, nz)
            for q in range(depth + 2):
                at = first + q
                yield q, recv_a[h][jnp.where(at >= nz, at - nz, at)]

        for j in reversed(range(1, nslab)):
            s = other(me, j, nslab)
            for q, plane in wanted(s):
                send_b[h][s, q] = plane
            b_copy(h, s, me).start()

        for q, plane in wanted(me):
            recv_b[h][me, q] = plane

    def wait_b(h):
        every(send_b[h].at[: nslab - 1], recv_b[h].at[: nslab - 1], r["b_s"], r["b_r"], h).wait_recv()

    def turn(c):
        for z in range(depth):
            turned = hbuf[c, z].T
            for q in range(chunks):
                ht[q, pl.ds(pl.multiple_of(c * CHUNK, CHUNK), CHUNK), z * nx : (z + 1) * nx] = turned[
                    q * CHUNK : (q + 1) * CHUNK
                ]

    def turn_beside(j):
        if j < ch:
            turn(j)

    def fill_taps():
        y_in = lax.broadcasted_iota(jnp.int32, (ny, ny), 0)
        y_out = lax.broadcasted_iota(jnp.int32, (ny, ny), 1)
        hits = [y_in == lax.rem(y_out - dy + ny, ny) for dy in (-1, 0, 1)]
        taps = weight[...].astype(F32)
        for k in range(27):
            wide[k] = jnp.broadcast_to(taps[:, k : k + 1], (ch, ny))

        def one(p, _):
            for cc in range(2):
                for j in range(9):
                    block = jnp.zeros((ny, ny), F32)
                    for d in range(3):
                        block = jnp.where(hits[d], wide[3 * j + d, pl.ds(2 * p + cc, 1)], block)
                    wmat[p, j * ny : (j + 1) * ny, cc * ny : (cc + 1) * ny] = block.astype(BF16)
            return 0

        lax.fori_loop(0, pairs, one, 0)

    for load in smalls:
        load.wait()
    planes[0].wait()
    weigh(0)
    pl.semaphore_wait(barrier, nslab - 1 + nbox - 1)
    send_z(0)
    for h in range(1, halves):
        planes[h].wait()
        weigh(h)
        send_z(h)

    fill_taps()
    h_copy.wait()
    merge_send(0, turn_beside)
    for c in range(nslab - 1, ch):
        turn(c)
    for h in range(1, halves):
        merge_send(h)
        wait_a(h - 1)
        turn_send(h - 1)
    wait_a(halves - 1)
    turn_send(halves - 1)
    for h in range(halves):
        wait_b(h)

    for q in range(depth + 2):
        plane = jnp.concatenate([recv_b[h][:, q].astype(F32).reshape(part, ny) for h in range(halves)], axis=0)
        for dx in (-1, 0, 1):
            moved = (plane if dx == 0 else pltpu.roll(plane, dx % nx, 0)).astype(BF16)
            for dz in (-1, 0, 1):
                z, j = q + dz - 1, (dz + 1) * 3 + dx + 1
                if 0 <= z < depth:
                    lmat[z * nx : (z + 1) * nx, j * ny : (j + 1) * ny] = moved
            turned = moved.T
            at = slice(q * nx, (q + 1) * nx)
            ft[dx + 1, EDGE : EDGE + ny, at] = turned
            ft[dx + 1, 0:EDGE, at] = turned[ny - EDGE : ny]
            ft[dx + 1, EDGE + ny : EDGE + ny + EDGE, at] = turned[0:EDGE]

    product = None
    for q in range(chunks):
        field = jnp.concatenate(
            [
                ft[dx + 1, q * CHUNK : q * CHUNK + window, (1 - dz) * nx : (1 - dz + depth) * nx]
                for dz in (-1, 0, 1)
                for dx in (-1, 0, 1)
            ],
            axis=0,
        )
        term = lax.dot_general(field, ht[q], NT, preferred_element_type=F32)
        product = term if product is None else product + term
    product = product.reshape(9, window, ch * CHUNK)
    w_row = lax.broadcasted_iota(jnp.int32, (window, ch * CHUNK), 0)
    w_y = lax.rem(lax.broadcasted_iota(jnp.int32, (window, ch * CHUNK), 1), CHUNK)
    picks = [w_row == w_y + EDGE - dy for dy in (-1, 0, 1)]
    sums = [
        jnp.sum(jnp.where(picks[d], product[j], 0.0), axis=0, keepdims=True) for j in range(9) for d in range(3)
    ]
    sums.append(jnp.zeros((5, ch * CHUNK), F32))
    by_tap = jnp.concatenate(sums, axis=0)
    by_channel = jnp.sum(by_tap.T.reshape(ch, CHUNK, 32), axis=1)
    by_channel = jnp.concatenate([by_channel, jnp.zeros((ch, 96), F32)], axis=1)
    of_four = lax.rem(lax.broadcasted_iota(jnp.int32, (ch, 128), 0), 4)
    packed = jnp.where(of_four == 0, by_channel, 0.0)
    for i in range(1, 4):
        packed = packed + pltpu.roll(jnp.where(of_four == i, by_channel, 0.0), 32 * i, 1)
    packed = jnp.sum(packed.reshape(ch // 4, 4, 128), axis=1)
    ndev = nbox * nslab
    my = g * nslab + me
    msg[...] = packed
    terms[my] = packed

    def r_copy(b, s, source):
        return pltpu.make_async_remote_copy(
            src_ref=msg,
            dst_ref=terms.at[source],
            send_sem=r["r_s"].at[0],
            recv_sem=r["r_r"].at[0],
            device_id={"box": b, "slab": s},
            device_id_type=MESH,
        )

    def send_r():
        for j in reversed(range(1, ndev)):
            r_copy(other(g, j // nslab, nbox), other(me, j % nslab, nslab), my).start()

    def pair_grads(p, _):
        grads = jnp.dot(lmat[...], wmat[p], preferred_element_type=F32)
        for cc in range(2):
            out[2 * p + cc] = grads[:, cc * ny : (cc + 1) * ny].reshape(depth, nx, ny).astype(BF16)
        return 0

    send_r()
    lax.fori_loop(0, pairs, pair_grads, 0)

    @pl.when(g < nbox - 1)
    def _():
        every(z_up, from_below, r["up_s"], r["up_s"], 0).wait_send()

    @pl.when(g > 0)
    def _():
        every(z_dn, from_above, r["dn_s"], r["dn_s"], 0).wait_send()

    for h in range(halves):
        every(send_a[h].at[: nslab - 1], recv_a[h].at[: (nslab - 1) * depth], r["a_s"], r["a_r"], h).wait_send()
        every(send_b[h].at[: nslab - 1], recv_b[h].at[: nslab - 1], r["b_s"], r["b_r"], h).wait_send()
    r_all = every(terms.at[: ndev - 1], terms.at[: ndev - 1], r["r_s"], r["r_r"], 0)
    r_all.wait_send()
    r_all.wait_recv()
    total = jnp.sum(terms[...], axis=0) * scale
    for c in range(ch):
        wg[c : c + 1, :] = total[c // 4 : c // 4 + 1, (c % 4) * 32 : (c % 4) * 32 + 27]


def write(grads, terms, out, wg, sem):
    copies = [pltpu.make_async_copy(terms, wg, sem.at[0])]
    copies += [pltpu.make_async_copy(grads.at[c], out.at[c], sem.at[c + 1]) for c in range(grads.shape[0])]
    for copy in copies:
        copy.start()
    for copy in copies:
        copy.wait()


def local(
    nbox,
    nslab,
    hidden_field,
    cone_grad,
    conv_weight,
    box_lower,
    box_upper,
    plane_lower,
    plane_upper,
    weight_lower,
    weight_upper,
):
    _, ch, depth, nx, ny = hidden_field.shape
    halves, rows = split(nx, nslab)
    nz = depth * nslab
    scale = 1.0 / math.sqrt(nbox * nz * nx * ny)
    vmem = pl.BlockSpec(memory_space=pltpu.VMEM)
    hbm = pl.BlockSpec(memory_space=pltpu.HBM)
    dma = pltpu.SemaphoreType.DMA
    ins = {
        "bl_hbm": box_lower,
        "bu_hbm": box_upper,
        "plo_hbm": plane_lower,
        "pup_hbm": plane_upper,
        "wl_hbm": weight_lower,
        "wu_hbm": weight_upper,
        "cone_hbm": cone_grad,
        "weight_hbm": conv_weight,
        "h_hbm": hidden_field.reshape(ch, depth, nx, ny),
    }
    chunk = (halves, nslab, depth, rows, ny)
    scratch = {n: pltpu.SMEM((depth,), jnp.int32) for n in ("bl", "bu", "plo", "pup", "wl", "wu")}
    scratch["cone"] = pltpu.VMEM(cone_grad.shape, F32)
    scratch["weight"] = pltpu.VMEM(conv_weight.shape, BF16)
    scratch["hbuf"] = pltpu.VMEM((ch, depth, nx, ny), BF16)
    scratch["own"] = pltpu.VMEM(chunk, F32)
    for n in ("z_up", "z_dn", "from_above", "from_below"):
        scratch[n] = pltpu.VMEM(chunk, BF16)
    for h in range(halves):
        scratch["send_a%d" % h] = pltpu.VMEM(chunk[1:], BF16)
        scratch["recv_a%d" % h] = pltpu.VMEM((nz, rows, ny), BF16)
        scratch["send_b%d" % h] = pltpu.VMEM((nslab, depth + 2, rows, ny), BF16)
        scratch["recv_b%d" % h] = pltpu.VMEM((nslab, depth + 2, rows, ny), BF16)
    scratch["ht"] = pltpu.VMEM((ny // CHUNK, ch * CHUNK, depth * nx), BF16)
    scratch["wide"] = pltpu.VMEM((27, ch, ny), F32)
    scratch["wmat"] = pltpu.VMEM((ch // 2, 9 * ny, 2 * ny), BF16)
    scratch["lmat"] = pltpu.VMEM((depth * nx, 9 * ny), BF16)
    scratch["ft"] = pltpu.VMEM((3, ny + 2 * EDGE, (depth + 2) * nx), BF16)
    scratch["msg"] = pltpu.VMEM((ch // 4, 128), F32)
    scratch["terms"] = pltpu.VMEM((nbox * nslab, ch // 4, 128), F32)
    scratch["isem"] = dma((7,))
    scratch["csem"] = dma((halves,))
    scratch["hsem"] = dma((1,))
    for n in ("up", "dn"):
        scratch[n + "_s"] = dma((1,))
        scratch[n + "_r"] = dma((halves, nslab))
    for n in ("a", "b"):
        scratch[n + "_s"] = dma((halves,))
        scratch[n + "_r"] = dma((halves,))
    scratch["r_s"] = dma((1,))
    scratch["r_r"] = dma((1,))
    names = (*ins, "out", "wg", *scratch)
    hidden_grad, weight_grad = pl.pallas_call(
        functools.partial(kernel, nbox, nslab, scale, names),
        out_shape=(
            pltpu.VMEM((ch, depth, nx, ny), BF16),
            pltpu.VMEM((ch, 27), F32),
        ),
        in_specs=[hbm] * len(ins),
        out_specs=(vmem, vmem),
        scratch_shapes=list(scratch.values()),
        compiler_params=pltpu.CompilerParams(
            collective_id=0, has_side_effects=True, vmem_limit_bytes=int(44 * 2**20)
        ),
    )(*(pltpu.with_memory_space_constraint(x, pltpu.HBM) for x in ins.values()))
    hidden_grad, weight_grad = pl.pallas_call(
        write,
        out_shape=(pltpu.HBM(hidden_grad.shape, BF16), pltpu.HBM(weight_grad.shape, F32)),
        in_specs=[vmem, vmem],
        out_specs=(hbm, hbm),
        scratch_shapes=[dma((ch + 1,))],
    )(pltpu.with_memory_space_constraint(hidden_grad, pltpu.VMEM), pltpu.with_memory_space_constraint(weight_grad, pltpu.VMEM))
    return hidden_grad.reshape(hidden_field.shape), weight_grad


def solution(mesh):
    in_specs = (
        P("box", None, "slab", None, None),
        P(("box", "slab"), None, None),
        P(),
        P(("box", "slab")),
        P(("box", "slab")),
        P(("box", "slab")),
        P(("box", "slab")),
        P(("box", "slab")),
        P(("box", "slab")),
    )
    out_specs = (P("box", None, "slab", None, None), P())
    return jax.shard_map(
        functools.partial(local, mesh.shape["box"], mesh.shape["slab"]),
        mesh=mesh,
        in_specs=in_specs,
        out_specs=out_specs,
        check_vma=False,
    )
```

```python
import functools
import math

import jax
import jax.numpy as jnp
from jax import lax
from jax.experimental import pallas as pl
from jax.experimental.pallas import tpu as pltpu
from jax.sharding import PartitionSpec as P

WDEN = 256
MESH = pl.DeviceIdType.MESH
F32 = jnp.float32
BF16 = jnp.bfloat16
CHUNK = 32
EDGE = 8
NT = (((1,), (1,)), ((), ()))


def split(nx, nslab):
    rows = nx // nslab
    halves = 2 if rows % 16 == 0 else 1
    return halves, rows // halves


def other(at, j, size):
    bit, partner = 1, at
    while bit < size:
        if j & bit:
            partner = partner + bit * (1 - 2 * lax.rem(lax.div(at, bit), 2))
        bit *= 2
    return partner


def kernel(nbox, nslab, scale, names, *refs):
    r = dict(zip(names, refs, strict=True))
    cone, weight, hbuf, out, wg = r["cone"], r["weight"], r["hbuf"], r["out"], r["wg"]
    bl, bu, plo, pup, wl, wu = (r[n] for n in ("bl", "bu", "plo", "pup", "wl", "wu"))
    own, z_up, z_dn = r["own"], r["z_up"], r["z_dn"]
    from_above, from_below = r["from_above"], r["from_below"]
    ht, wide, wmat, lmat, ft = r["ht"], r["wide"], r["wmat"], r["lmat"], r["ft"]
    msg, terms = r["msg"], r["terms"]

    g = lax.axis_index("box")
    me = lax.axis_index("slab")
    depth, nx, ny = cone.shape
    halves, rows = split(nx, nslab)
    part = nx // halves
    nz = depth * nslab
    ch = hbuf.shape[0]
    pairs = ch // 2
    chunks = ny // CHUNK
    window = CHUNK + 2 * EDGE
    send_a = [r["send_a%d" % h] for h in range(halves)]
    recv_a = [r["recv_a%d" % h] for h in range(halves)]
    send_b = [r["send_b%d" % h] for h in range(halves)]
    recv_b = [r["recv_b%d" % h] for h in range(halves)]

    smalls = [
        pltpu.make_async_copy(r[n + "_hbm"], r[n], r["isem"].at[i])
        for i, n in enumerate(("bl", "bu", "wl", "wu", "plo", "pup", "weight"))
    ]
    planes = [
        pltpu.make_async_copy(
            r["cone_hbm"].at[:, h * part : (h + 1) * part],
            cone.at[:, h * part : (h + 1) * part],
            r["csem"].at[h],
        )
        for h in range(halves)
    ]
    h_copy = pltpu.make_async_copy(r["h_hbm"], hbuf, r["hsem"].at[0])
    planes[0].start()
    for load in smalls:
        load.start()
    for load in planes[1:]:
        load.start()
    h_copy.start()

    barrier = pltpu.get_barrier_semaphore()

    def greet_slab(j, _):
        pl.semaphore_signal(barrier, inc=1, device_id={"slab": lax.rem(me + j, nslab)}, device_id_type=MESH)
        return 0

    def greet_box(j, _):
        pl.semaphore_signal(barrier, inc=1, device_id={"box": lax.rem(g + j, nbox)}, device_id_type=MESH)
        return 0

    lax.fori_loop(1, nslab, greet_slab, 0)
    lax.fori_loop(1, nbox, greet_box, 0)

    def weigh(h):
        for i in range(depth):
            below_c = jnp.where(bl[i] == g - 1, wl[i].astype(F32) * (1.0 / WDEN), 0.0)
            above_c = jnp.where(bu[i] == g + 1, wu[i].astype(F32) * (1.0 / WDEN), 0.0)
            plane = cone[i, h * part : (h + 1) * part].reshape(nslab, rows, ny)
            z_up[h, :, i] = (above_c * plane).astype(BF16)
            z_dn[h, :, i] = (below_c * plane).astype(BF16)

    def weigh_own(i, _):
        lower = wl[i].astype(F32) * (1.0 / WDEN)
        upper = wu[i].astype(F32) * (1.0 / WDEN)
        own_c = jnp.where(bl[i] == g, lower, 0.0) + jnp.where(bu[i] == g, upper, 0.0)
        own[:, :, i] = own_c * cone[i].reshape(halves, nslab, rows, ny)
        return 0

    def every(source, target, send, recv, at):
        return pltpu.make_async_remote_copy(
            src_ref=source,
            dst_ref=target,
            send_sem=send.at[at],
            recv_sem=recv.at[at],
            device_id={"slab": me},
            device_id_type=MESH,
        )

    def up_copy(h, c):
        return pltpu.make_async_remote_copy(
            src_ref=z_up.at[h, pl.ds(2 * c, 2)],
            dst_ref=from_below.at[h, pl.ds(2 * c, 2)],
            send_sem=r["up_s"].at[0],
            recv_sem=r["up_r"].at[h, c],
            device_id={"box": lax.rem(g + 1, nbox)},
            device_id_type=MESH,
        )

    def dn_copy(h, c):
        return pltpu.make_async_remote_copy(
            src_ref=z_dn.at[h, pl.ds(2 * c, 2)],
            dst_ref=from_above.at[h, pl.ds(2 * c, 2)],
            send_sem=r["dn_s"].at[0],
            recv_sem=r["dn_r"].at[h, c],
            device_id={"box": lax.rem(g + nbox - 1, nbox)},
            device_id_type=MESH,
        )

    chips = [other(lax.div(me, 2), j, nslab // 2) for j in reversed(range(nslab // 2))]

    def send_z(h, which):
        for c in which:

            @pl.when(g < nbox - 1)
            def _():
                up_copy(h, c).start()

            @pl.when(g > 0)
            def _():
                dn_copy(h, c).start()

    def a_copy(h, t, source):
        return pltpu.make_async_remote_copy(
            src_ref=send_a[h].at[t],
            dst_ref=recv_a[h].at[pl.ds(source * depth, depth)],
            send_sem=r["a_s"].at[h],
            recv_sem=r["a_r"].at[h],
            device_id={"slab": t},
            device_id_type=MESH,
        )

    def merge_send(h, which, beside=None):
        sibling = other(me, 1, nslab)
        for n, c in which:

            @pl.when(g < nbox - 1)
            def _():
                dn_copy(h, c).wait_recv()

            @pl.when(g > 0)
            def _():
                up_copy(h, c).wait_recv()

            def merged(t):
                return (own[h, t] + from_above[h, t].astype(F32) + from_below[h, t].astype(F32)).astype(BF16)

            last = n == len(chips) - 1
            for t in (sibling, me) if last else (2 * c, 2 * c + 1):
                if last and t is me:
                    recv_a[h][pl.ds(me * depth, depth)] = merged(me)
                else:
                    send_a[h][t] = merged(t)
                    a_copy(h, t, me).start()
            if beside is not None:
                beside(n)

    def wait_a(h):
        every(send_a[h].at[: nslab - 1], recv_a[h].at[: (nslab - 1) * depth], r["a_s"], r["a_r"], h).wait_recv()

    def b_copy(h, s, source):
        return pltpu.make_async_remote_copy(
            src_ref=send_b[h].at[s],
            dst_ref=recv_b[h].at[source],
            send_sem=r["b_s"].at[h],
            recv_sem=r["b_r"].at[h],
            device_id={"slab": s},
            device_id_type=MESH,
        )

    def turn_send(h):
        offset = jnp.where(bl[0] == g, plo[0], pup[0]) - me * depth

        recv_a[h][nz:] = recv_a[h][: depth + 2]

        def wanted(s):
            return recv_a[h][pl.ds(lax.rem(s * depth - 1 - offset + 2 * nz, nz), depth + 2)]

        for j in reversed(range(1, nslab)):
            s = other(me, j, nslab)
            send_b[h][s] = wanted(s)
            b_copy(h, s, me).start()
        recv_b[h][me] = wanted(me)

    def wait_b(h):
        every(send_b[h].at[: nslab - 1], recv_b[h].at[: nslab - 1], r["b_s"], r["b_r"], h).wait_recv()

    def turn(c):
        for z in range(depth):
            turned = hbuf[c, z].T
            for q in range(chunks):
                ht[q, pl.ds(pl.multiple_of(c * CHUNK, CHUNK), CHUNK), z * nx : (z + 1) * nx] = turned[
                    q * CHUNK : (q + 1) * CHUNK
                ]

    def turn_beside(n):
        for c in range(n * ch // len(chips), (n + 1) * ch // len(chips)):
            turn(c)

    def fill_taps():
        y_in = lax.broadcasted_iota(jnp.int32, (ny, ny), 0)
        y_out = lax.broadcasted_iota(jnp.int32, (ny, ny), 1)
        hits = [y_in == lax.rem(y_out - dy + ny, ny) for dy in (-1, 0, 1)]
        taps = weight[...].astype(F32)
        for k in range(27):
            wide[k] = jnp.broadcast_to(taps[:, k : k + 1], (ch, ny))

        def one(p, _):
            for cc in range(2):
                for j in range(9):
                    block = jnp.zeros((ny, ny), F32)
                    for d in range(3):
                        block = jnp.where(hits[d], wide[3 * j + d, pl.ds(2 * p + cc, 1)], block)
                    wmat[p, j * ny : (j + 1) * ny, cc * ny : (cc + 1) * ny] = block.astype(BF16)
            return 0

        lax.fori_loop(0, pairs, one, 0)

    for load in smalls:
        load.wait()
    planes[0].wait()
    weigh(0)
    pl.semaphore_wait(barrier, nslab - 1 + nbox - 1)
    send_z(0, chips[:-1])
    for h in range(1, halves):
        planes[h].wait()
        weigh(h)
        send_z(h, chips[:-1])
    for h in range(halves):
        send_z(h, chips[-1:])

    lax.fori_loop(0, depth, weigh_own, 0)

    @pl.when(g == nbox - 1)
    def _():
        from_above[...] = jnp.zeros_like(from_above)

    @pl.when(g == 0)
    def _():
        from_below[...] = jnp.zeros_like(from_below)

    fill_taps()
    h_copy.wait()
    order = list(enumerate(chips))
    merge_send(0, order[:-1], turn_beside)
    turn_beside(len(chips) - 1)
    for h in range(1, halves):
        merge_send(h, order[:-1])
    for h in range(halves):
        merge_send(h, order[-1:])
    for h in range(halves - 1):
        wait_a(h)
        turn_send(h)
    wait_a(halves - 1)
    turn_send(halves - 1)
    for h in range(halves):
        wait_b(h)

    def moved(q, dx):
        plane = jnp.concatenate([recv_b[h][:, q].astype(F32).reshape(part, ny) for h in range(halves)], axis=0)
        return (plane if dx == 0 else pltpu.roll(plane, dx % nx, 0)).astype(BF16)

    for q in range(depth + 2):
        for dx in (-1, 0, 1):
            turned = moved(q, dx).T
            at = slice(q * nx, (q + 1) * nx)
            ft[dx + 1, EDGE : EDGE + ny, at] = turned
            ft[dx + 1, 0:EDGE, at] = turned[ny - EDGE : ny]
            ft[dx + 1, EDGE + ny : EDGE + ny + EDGE, at] = turned[0:EDGE]

    product = None
    for q in range(chunks):
        field = jnp.concatenate(
            [
                ft[dx + 1, q * CHUNK : q * CHUNK + window, (1 - dz) * nx : (1 - dz + depth) * nx]
                for dz in (-1, 0, 1)
                for dx in (-1, 0, 1)
            ],
            axis=0,
        )
        term = lax.dot_general(field, ht[q], NT, preferred_element_type=F32)
        product = term if product is None else product + term
    product = product.reshape(9, window, ch * CHUNK)
    w_row = lax.broadcasted_iota(jnp.int32, (window, ch * CHUNK), 0)
    w_y = lax.rem(lax.broadcasted_iota(jnp.int32, (window, ch * CHUNK), 1), CHUNK)
    picks = [w_row == w_y + EDGE - dy for dy in (-1, 0, 1)]
    sums = [
        jnp.sum(jnp.where(picks[d], product[j], 0.0), axis=0, keepdims=True) for j in range(9) for d in range(3)
    ]
    sums.append(jnp.zeros((5, ch * CHUNK), F32))
    by_tap = jnp.concatenate(sums, axis=0)
    by_channel = jnp.sum(by_tap.T.reshape(ch, CHUNK, 32), axis=1)
    by_channel = jnp.concatenate([by_channel, jnp.zeros((ch, 96), F32)], axis=1)
    of_four = lax.rem(lax.broadcasted_iota(jnp.int32, (ch, 128), 0), 4)
    packed = jnp.where(of_four == 0, by_channel, 0.0)
    for i in range(1, 4):
        packed = packed + pltpu.roll(jnp.where(of_four == i, by_channel, 0.0), 32 * i, 1)
    packed = jnp.sum(packed.reshape(ch // 4, 4, 128), axis=1)
    ndev = nbox * nslab
    my = g * nslab + me
    msg[...] = packed
    terms[my] = packed

    def r_copy(b, s, source):
        return pltpu.make_async_remote_copy(
            src_ref=msg,
            dst_ref=terms.at[source],
            send_sem=r["r_s"].at[0],
            recv_sem=r["r_r"].at[0],
            device_id={"box": b, "slab": s},
            device_id_type=MESH,
        )

    def send_r():
        for j in reversed(range(1, ndev)):
            r_copy(other(g, j // nslab, nbox), other(me, j % nslab, nslab), my).start()

    def pair_grads(p, _):
        grads = jnp.dot(lmat[...], wmat[p], preferred_element_type=F32)
        for cc in range(2):
            out[2 * p + cc] = grads[:, cc * ny : (cc + 1) * ny].reshape(depth, nx, ny).astype(BF16)
        return 0

    send_r()
    for q in range(depth + 2):
        for dx in (-1, 0, 1):
            plane = moved(q, dx)
            for dz in (-1, 0, 1):
                z, j = q + dz - 1, (dz + 1) * 3 + dx + 1
                if 0 <= z < depth:
                    lmat[z * nx : (z + 1) * nx, j * ny : (j + 1) * ny] = plane
    lax.fori_loop(0, pairs, pair_grads, 0)

    @pl.when(g < nbox - 1)
    def _():
        every(z_up, from_below, r["up_s"], r["up_s"], 0).wait_send()

    @pl.when(g > 0)
    def _():
        every(z_dn, from_above, r["dn_s"], r["dn_s"], 0).wait_send()

    for h in range(halves):
        every(send_a[h].at[: nslab - 1], recv_a[h].at[: (nslab - 1) * depth], r["a_s"], r["a_r"], h).wait_send()
        every(send_b[h].at[: nslab - 1], recv_b[h].at[: nslab - 1], r["b_s"], r["b_r"], h).wait_send()
    r_all = every(terms.at[: ndev - 1], terms.at[: ndev - 1], r["r_s"], r["r_r"], 0)
    r_all.wait_send()
    r_all.wait_recv()
    total = jnp.sum(terms[...], axis=0) * scale
    for c in range(ch):
        wg[c : c + 1, :] = total[c // 4 : c // 4 + 1, (c % 4) * 32 : (c % 4) * 32 + 27]


def write(grads, terms, out, wg, sem):
    copies = [pltpu.make_async_copy(terms, wg, sem.at[0])]
    copies += [pltpu.make_async_copy(grads.at[c], out.at[c], sem.at[c + 1]) for c in range(grads.shape[0])]
    for copy in copies:
        copy.start()
    for copy in copies:
        copy.wait()


def local(
    nbox,
    nslab,
    hidden_field,
    cone_grad,
    conv_weight,
    box_lower,
    box_upper,
    plane_lower,
    plane_upper,
    weight_lower,
    weight_upper,
):
    _, ch, depth, nx, ny = hidden_field.shape
    halves, rows = split(nx, nslab)
    nz = depth * nslab
    scale = 1.0 / math.sqrt(nbox * nz * nx * ny)
    vmem = pl.BlockSpec(memory_space=pltpu.VMEM)
    hbm = pl.BlockSpec(memory_space=pltpu.HBM)
    dma = pltpu.SemaphoreType.DMA
    ins = {
        "bl_hbm": box_lower,
        "bu_hbm": box_upper,
        "plo_hbm": plane_lower,
        "pup_hbm": plane_upper,
        "wl_hbm": weight_lower,
        "wu_hbm": weight_upper,
        "cone_hbm": cone_grad,
        "weight_hbm": conv_weight,
        "h_hbm": hidden_field.reshape(ch, depth, nx, ny),
    }
    chunk = (halves, nslab, depth, rows, ny)
    scratch = {n: pltpu.SMEM((depth,), jnp.int32) for n in ("bl", "bu", "plo", "pup", "wl", "wu")}
    scratch["cone"] = pltpu.VMEM(cone_grad.shape, F32)
    scratch["weight"] = pltpu.VMEM(conv_weight.shape, BF16)
    scratch["hbuf"] = pltpu.VMEM((ch, depth, nx, ny), BF16)
    scratch["own"] = pltpu.VMEM(chunk, F32)
    for n in ("z_up", "z_dn", "from_above", "from_below"):
        scratch[n] = pltpu.VMEM(chunk, BF16)
    for h in range(halves):
        scratch["send_a%d" % h] = pltpu.VMEM(chunk[1:], BF16)
        scratch["recv_a%d" % h] = pltpu.VMEM((nz + depth + 2, rows, ny), BF16)
        scratch["send_b%d" % h] = pltpu.VMEM((nslab, depth + 2, rows, ny), BF16)
        scratch["recv_b%d" % h] = pltpu.VMEM((nslab, depth + 2, rows, ny), BF16)
    scratch["ht"] = pltpu.VMEM((ny // CHUNK, ch * CHUNK, depth * nx), BF16)
    scratch["wide"] = pltpu.VMEM((27, ch, ny), F32)
    scratch["wmat"] = pltpu.VMEM((ch // 2, 9 * ny, 2 * ny), BF16)
    scratch["lmat"] = pltpu.VMEM((depth * nx, 9 * ny), BF16)
    scratch["ft"] = pltpu.VMEM((3, ny + 2 * EDGE, (depth + 2) * nx), BF16)
    scratch["msg"] = pltpu.VMEM((ch // 4, 128), F32)
    scratch["terms"] = pltpu.VMEM((nbox * nslab, ch // 4, 128), F32)
    scratch["isem"] = dma((7,))
    scratch["csem"] = dma((halves,))
    scratch["hsem"] = dma((1,))
    for n in ("up", "dn"):
        scratch[n + "_s"] = dma((1,))
        scratch[n + "_r"] = dma((halves, nslab // 2))
    for n in ("a", "b"):
        scratch[n + "_s"] = dma((halves,))
        scratch[n + "_r"] = dma((halves,))
    scratch["r_s"] = dma((1,))
    scratch["r_r"] = dma((1,))
    names = (*ins, "out", "wg", *scratch)
    hidden_grad, weight_grad = pl.pallas_call(
        functools.partial(kernel, nbox, nslab, scale, names),
        out_shape=(
            pltpu.VMEM((ch, depth, nx, ny), BF16),
            pltpu.VMEM((ch, 27), F32),
        ),
        in_specs=[hbm] * len(ins),
        out_specs=(vmem, vmem),
        scratch_shapes=list(scratch.values()),
        compiler_params=pltpu.CompilerParams(
            collective_id=0, has_side_effects=True, vmem_limit_bytes=int(44 * 2**20)
        ),
    )(*(pltpu.with_memory_space_constraint(x, pltpu.HBM) for x in ins.values()))
    hidden_grad, weight_grad = pl.pallas_call(
        write,
        out_shape=(pltpu.HBM(hidden_grad.shape, BF16), pltpu.HBM(weight_grad.shape, F32)),
        in_specs=[vmem, vmem],
        out_specs=(hbm, hbm),
        scratch_shapes=[dma((ch + 1,))],
    )(pltpu.with_memory_space_constraint(hidden_grad, pltpu.VMEM), pltpu.with_memory_space_constraint(weight_grad, pltpu.VMEM))
    return hidden_grad.reshape(hidden_field.shape), weight_grad


def solution(mesh):
    in_specs = (
        P("box", None, "slab", None, None),
        P(("box", "slab"), None, None),
        P(),
        P(("box", "slab")),
        P(("box", "slab")),
        P(("box", "slab")),
        P(("box", "slab")),
        P(("box", "slab")),
        P(("box", "slab")),
    )
    out_specs = (P("box", None, "slab", None, None), P())
    return jax.shard_map(
        functools.partial(local, mesh.shape["box"], mesh.shape["slab"]),
        mesh=mesh,
        in_specs=in_specs,
        out_specs=out_specs,
        check_vma=False,
    )
```

```python
import functools
import math

import jax
import jax.numpy as jnp
from jax import lax
from jax.experimental import pallas as pl
from jax.experimental.pallas import tpu as pltpu
from jax.sharding import PartitionSpec as P

WDEN = 256
MESH = pl.DeviceIdType.MESH
F32 = jnp.float32
BF16 = jnp.bfloat16
CHUNK = 32
EDGE = 8


def split(nx, nslab):
    rows = nx // nslab
    halves = 2 if rows % 16 == 0 else 1
    return halves, rows // halves


def other(at, j, size):
    bit, partner = 1, at
    while bit < size:
        if j & bit:
            partner = partner + bit * (1 - 2 * lax.rem(lax.div(at, bit), 2))
        bit *= 2
    return partner


def kernel(nbox, nslab, scale, names, *refs):
    r = dict(zip(names, refs, strict=True))
    cone, weight, hbuf, out, wg = r["cone"], r["weight"], r["hbuf"], r["out"], r["wg"]
    bl, bu, plo, pup, wl, wu = (r[n] for n in ("bl", "bu", "plo", "pup", "wl", "wu"))
    own, z_up, z_dn = r["own"], r["z_up"], r["z_dn"]
    from_above, from_below = r["from_above"], r["from_below"]
    shifted, wide, wmat, lmat, product = r["shifted"], r["wide"], r["wmat"], r["lmat"], r["product"]
    msg, terms = r["msg"], r["terms"]

    g = lax.axis_index("box")
    me = lax.axis_index("slab")
    depth, nx, ny = cone.shape
    halves, rows = split(nx, nslab)
    part = nx // halves
    nz = depth * nslab
    ch = hbuf.shape[0]
    pairs = ch // 2
    chunks = ny // CHUNK
    window = CHUNK + 2 * EDGE
    wide_n = ch * CHUNK
    send_a = [r["send_a%d" % h] for h in range(halves)]
    recv_a = [r["recv_a%d" % h] for h in range(halves)]
    send_b = [r["send_b%d" % h] for h in range(halves)]
    recv_b = [r["recv_b%d" % h] for h in range(halves)]

    smalls = [
        pltpu.make_async_copy(r[n + "_hbm"], r[n], r["isem"].at[i])
        for i, n in enumerate(("bl", "bu", "wl", "wu", "plo", "pup", "weight"))
    ]
    planes = [
        pltpu.make_async_copy(
            r["cone_hbm"].at[:, h * part : (h + 1) * part],
            cone.at[:, h * part : (h + 1) * part],
            r["csem"].at[h],
        )
        for h in range(halves)
    ]
    h_copy = pltpu.make_async_copy(r["h_hbm"], hbuf, r["hsem"].at[0])
    planes[0].start()
    for load in smalls:
        load.start()
    for load in planes[1:]:
        load.start()
    h_copy.start()

    barrier = pltpu.get_barrier_semaphore()

    def greet_slab(j, _):
        pl.semaphore_signal(barrier, inc=1, device_id={"slab": lax.rem(me + j, nslab)}, device_id_type=MESH)
        return 0

    def greet_box(j, _):
        pl.semaphore_signal(barrier, inc=1, device_id={"box": lax.rem(g + j, nbox)}, device_id_type=MESH)
        return 0

    lax.fori_loop(1, nslab, greet_slab, 0)
    lax.fori_loop(1, nbox, greet_box, 0)

    def weigh(h):
        for i in range(depth):
            below_c = jnp.where(bl[i] == g - 1, wl[i].astype(F32) * (1.0 / WDEN), 0.0)
            above_c = jnp.where(bu[i] == g + 1, wu[i].astype(F32) * (1.0 / WDEN), 0.0)
            plane = cone[i, h * part : (h + 1) * part].reshape(nslab, rows, ny)
            z_up[h, :, i] = (above_c * plane).astype(BF16)
            z_dn[h, :, i] = (below_c * plane).astype(BF16)

    def weigh_own(i, _):
        lower = wl[i].astype(F32) * (1.0 / WDEN)
        upper = wu[i].astype(F32) * (1.0 / WDEN)
        own_c = jnp.where(bl[i] == g, lower, 0.0) + jnp.where(bu[i] == g, upper, 0.0)
        own[:, :, i] = own_c * cone[i].reshape(halves, nslab, rows, ny)
        return 0

    def every(source, target, send, recv, at):
        return pltpu.make_async_remote_copy(
            src_ref=source,
            dst_ref=target,
            send_sem=send.at[at],
            recv_sem=recv.at[at],
            device_id={"slab": me},
            device_id_type=MESH,
        )

    def up_copy(h, c):
        return pltpu.make_async_remote_copy(
            src_ref=z_up.at[h, pl.ds(2 * c, 2)],
            dst_ref=from_below.at[h, pl.ds(2 * c, 2)],
            send_sem=r["up_s"].at[0],
            recv_sem=r["up_r"].at[h, c],
            device_id={"box": lax.rem(g + 1, nbox)},
            device_id_type=MESH,
        )

    def dn_copy(h, c):
        return pltpu.make_async_remote_copy(
            src_ref=z_dn.at[h, pl.ds(2 * c, 2)],
            dst_ref=from_above.at[h, pl.ds(2 * c, 2)],
            send_sem=r["dn_s"].at[0],
            recv_sem=r["dn_r"].at[h, c],
            device_id={"box": lax.rem(g + nbox - 1, nbox)},
            device_id_type=MESH,
        )

    chips = [other(lax.div(me, 2), j, nslab // 2) for j in reversed(range(nslab // 2))]

    def send_z(h, which):
        for c in which:

            @pl.when(g < nbox - 1)
            def _():
                up_copy(h, c).start()

            @pl.when(g > 0)
            def _():
                dn_copy(h, c).start()

    def a_copy(h, t, source):
        return pltpu.make_async_remote_copy(
            src_ref=send_a[h].at[t],
            dst_ref=recv_a[h].at[pl.ds(source * depth, depth)],
            send_sem=r["a_s"].at[h],
            recv_sem=r["a_r"].at[h],
            device_id={"slab": t},
            device_id_type=MESH,
        )

    def merge_send(h, which):
        sibling = other(me, 1, nslab)
        for n, c in which:

            @pl.when(g < nbox - 1)
            def _():
                dn_copy(h, c).wait_recv()

            @pl.when(g > 0)
            def _():
                up_copy(h, c).wait_recv()

            def merged(t):
                return (own[h, t] + from_above[h, t].astype(F32) + from_below[h, t].astype(F32)).astype(BF16)

            last = n == len(chips) - 1
            for t in (sibling, me) if last else (2 * c, 2 * c + 1):
                if last and t is me:
                    recv_a[h][pl.ds(me * depth, depth)] = merged(me)
                else:
                    send_a[h][t] = merged(t)
                    a_copy(h, t, me).start()
    def wait_a(h):
        every(send_a[h].at[: nslab - 1], recv_a[h].at[: (nslab - 1) * depth], r["a_s"], r["a_r"], h).wait_recv()

    def b_copy(h, s, source):
        return pltpu.make_async_remote_copy(
            src_ref=send_b[h].at[s],
            dst_ref=recv_b[h].at[source],
            send_sem=r["b_s"].at[h],
            recv_sem=r["b_r"].at[h],
            device_id={"slab": s},
            device_id_type=MESH,
        )

    def turn_send(h):
        offset = jnp.where(bl[0] == g, plo[0], pup[0]) - me * depth

        recv_a[h][nz:] = recv_a[h][: depth + 2]

        def wanted(s):
            return recv_a[h][pl.ds(lax.rem(s * depth - 1 - offset + 2 * nz, nz), depth + 2)]

        for j in reversed(range(1, nslab)):
            s = other(me, j, nslab)
            send_b[h][s] = wanted(s)
            b_copy(h, s, me).start()
        recv_b[h][me] = wanted(me)

    def wait_b(h):
        every(send_b[h].at[: nslab - 1], recv_b[h].at[: nslab - 1], r["b_s"], r["b_r"], h).wait_recv()

    def shift(z, _):
        turned = [hbuf[c, z].T for c in range(ch)]
        for q in range(chunks):
            lanes = jnp.concatenate([t[q * CHUNK : (q + 1) * CHUNK] for t in turned], axis=0).T.astype(F32)
            for dx in (-1, 0, 1):
                rolled = (lanes if dx == 0 else pltpu.roll(lanes, -dx % nx, 0)).astype(BF16)
                for h in range(halves):
                    shifted[
                        h, q, pl.ds(pl.multiple_of(z * part, part), part), (dx + 1) * wide_n : (dx + 2) * wide_n
                    ] = rolled[h * part : (h + 1) * part]
        return 0

    def turn_field(h):
        for p in range(depth + 2):
            if part % 128 == 0:
                turned, at, ft = recv_b[h][:, p].astype(F32).reshape(part, ny).astype(BF16).T, p * part, r["ft0"]
            elif p <= depth:
                two = [recv_b[h][:, p + i].astype(F32).reshape(part, ny) for i in range(2)]
                turned = jnp.concatenate(two, axis=0).astype(BF16).T
                at, ft = (p - p % 2) * part, r["ft%d" % (p % 2)]
            else:
                continue
            at = slice(at, at + turned.shape[1])
            ft[EDGE : EDGE + ny, at] = turned
            ft[0:EDGE, at] = turned[ny - EDGE : ny]
            ft[EDGE + ny : EDGE + ny + EDGE, at] = turned[0:EDGE]

    def planes_from(p, q):
        odd = 0 if part % 128 == 0 else p % 2
        return r["ft%d" % odd][q * CHUNK : q * CHUNK + window, (p - odd) * part : (p - odd + depth) * part]

    def part_product(h):
        turn_field(h)
        total = None
        for q in range(chunks):
            field = jnp.concatenate([planes_from(1 - dz, q) for dz in (-1, 0, 1)], axis=0)
            term = jnp.dot(field, shifted[h, q], preferred_element_type=F32)
            total = term if total is None else total + term
        return total

    def fill_taps():
        y_in = lax.broadcasted_iota(jnp.int32, (ny, ny), 0)
        y_out = lax.broadcasted_iota(jnp.int32, (ny, ny), 1)
        hits = [y_in == lax.rem(y_out - dy + ny, ny) for dy in (-1, 0, 1)]
        taps = weight[...].astype(F32)
        for k in range(27):
            wide[k] = jnp.broadcast_to(taps[:, k : k + 1], (ch, ny))

        def one(p, _):
            for cc in range(2):
                for j in range(9):
                    block = jnp.zeros((ny, ny), F32)
                    for d in range(3):
                        block = jnp.where(hits[d], wide[3 * j + d, pl.ds(2 * p + cc, 1)], block)
                    wmat[p, j * ny : (j + 1) * ny, cc * ny : (cc + 1) * ny] = block.astype(BF16)
            return 0

        lax.fori_loop(0, pairs, one, 0)

    for load in smalls:
        load.wait()
    planes[0].wait()
    weigh(0)
    pl.semaphore_wait(barrier, nslab - 1 + nbox - 1)
    send_z(0, chips[:-1])
    for h in range(1, halves):
        planes[h].wait()
        weigh(h)
        send_z(h, chips[:-1])
    for h in range(halves):
        send_z(h, chips[-1:])

    lax.fori_loop(0, depth, weigh_own, 0)

    @pl.when(g == nbox - 1)
    def _():
        from_above[...] = jnp.zeros_like(from_above)

    @pl.when(g == 0)
    def _():
        from_below[...] = jnp.zeros_like(from_below)

    fill_taps()
    h_copy.wait()
    lax.fori_loop(0, depth // 2, shift, 0)
    order = list(enumerate(chips))
    merge_send(0, order[:-1])
    for h in range(1, halves):
        merge_send(h, order[:-1])
    for h in range(halves):
        merge_send(h, order[-1:])
    for h in range(halves - 1):
        wait_a(h)
        turn_send(h)
    wait_a(halves - 1)
    turn_send(halves - 1)
    lax.fori_loop(depth // 2, depth, shift, 0)
    for h in range(halves - 1):
        wait_b(h)
        product[...] = part_product(h) if h == 0 else product[...] + part_product(h)
    wait_b(halves - 1)
    sums = part_product(halves - 1)
    if halves > 1:
        sums = sums + product[...]
    sums = sums.reshape(3, window, 3 * wide_n)

    def moved(q, dx):
        plane = jnp.concatenate([recv_b[h][:, q].astype(F32).reshape(part, ny) for h in range(halves)], axis=0)
        return (plane if dx == 0 else pltpu.roll(plane, dx % nx, 0)).astype(BF16)

    w_row = lax.broadcasted_iota(jnp.int32, (window, 3 * wide_n), 0)
    w_y = lax.rem(lax.broadcasted_iota(jnp.int32, (window, 3 * wide_n), 1), CHUNK)
    picks = [w_row == w_y + EDGE - dy for dy in (-1, 0, 1)]
    by_tap = []
    for z in range(3):
        by_tap += [jnp.sum(jnp.where(pick, sums[z], 0.0), axis=0, keepdims=True) for pick in picks]
        by_tap.append(jnp.zeros((6 if z < 2 else 11, 3 * wide_n), F32))
    by_tap = jnp.sum(jnp.concatenate(by_tap, axis=0).T.reshape(3, ch, CHUNK, 32), axis=2)
    by_tap = jnp.concatenate([by_tap, jnp.zeros((3, ch, 96), F32)], axis=2)
    by_channel = by_tap[0] + pltpu.roll(by_tap[1], 3, 1) + pltpu.roll(by_tap[2], 6, 1)
    of_four = lax.rem(lax.broadcasted_iota(jnp.int32, (ch, 128), 0), 4)
    packed = jnp.where(of_four == 0, by_channel, 0.0)
    for i in range(1, 4):
        packed = packed + pltpu.roll(jnp.where(of_four == i, by_channel, 0.0), 32 * i, 1)
    packed = jnp.sum(packed.reshape(ch // 4, 4, 128), axis=1)
    ndev = nbox * nslab
    my = g * nslab + me
    msg[...] = packed
    terms[my] = packed

    def r_copy(b, s, source):
        return pltpu.make_async_remote_copy(
            src_ref=msg,
            dst_ref=terms.at[source],
            send_sem=r["r_s"].at[0],
            recv_sem=r["r_r"].at[0],
            device_id={"box": b, "slab": s},
            device_id_type=MESH,
        )

    def send_r():
        for j in reversed(range(1, ndev)):
            r_copy(other(g, j // nslab, nbox), other(me, j % nslab, nslab), my).start()

    def pair_grads(p, _):
        grads = jnp.dot(lmat[...], wmat[p], preferred_element_type=F32)
        for cc in range(2):
            out[2 * p + cc] = grads[:, cc * ny : (cc + 1) * ny].reshape(depth, nx, ny).astype(BF16)
        return 0

    send_r()
    for q in range(depth + 2):
        for dx in (-1, 0, 1):
            plane = moved(q, dx)
            for dz in (-1, 0, 1):
                z, j = q + dz - 1, (dz + 1) * 3 + dx + 1
                if 0 <= z < depth:
                    lmat[z * nx : (z + 1) * nx, j * ny : (j + 1) * ny] = plane
    lax.fori_loop(0, pairs, pair_grads, 0)

    @pl.when(g < nbox - 1)
    def _():
        every(z_up, from_below, r["up_s"], r["up_s"], 0).wait_send()

    @pl.when(g > 0)
    def _():
        every(z_dn, from_above, r["dn_s"], r["dn_s"], 0).wait_send()

    for h in range(halves):
        every(send_a[h].at[: nslab - 1], recv_a[h].at[: (nslab - 1) * depth], r["a_s"], r["a_r"], h).wait_send()
        every(send_b[h].at[: nslab - 1], recv_b[h].at[: nslab - 1], r["b_s"], r["b_r"], h).wait_send()
    r_all = every(terms.at[: ndev - 1], terms.at[: ndev - 1], r["r_s"], r["r_r"], 0)
    r_all.wait_send()
    r_all.wait_recv()
    total = jnp.sum(terms[...], axis=0) * scale
    for c in range(ch):
        wg[c : c + 1, :] = total[c // 4 : c // 4 + 1, (c % 4) * 32 : (c % 4) * 32 + 27]


def write(grads, terms, out, wg, sem):
    copies = [pltpu.make_async_copy(terms, wg, sem.at[0]), pltpu.make_async_copy(grads, out, sem.at[1])]
    for copy in copies:
        copy.start()
    for copy in copies:
        copy.wait()


def local(
    nbox,
    nslab,
    hidden_field,
    cone_grad,
    conv_weight,
    box_lower,
    box_upper,
    plane_lower,
    plane_upper,
    weight_lower,
    weight_upper,
):
    _, ch, depth, nx, ny = hidden_field.shape
    halves, rows = split(nx, nslab)
    nz = depth * nslab
    scale = 1.0 / math.sqrt(nbox * nz * nx * ny)
    vmem = pl.BlockSpec(memory_space=pltpu.VMEM)
    hbm = pl.BlockSpec(memory_space=pltpu.HBM)
    dma = pltpu.SemaphoreType.DMA
    ins = {
        "bl_hbm": box_lower,
        "bu_hbm": box_upper,
        "plo_hbm": plane_lower,
        "pup_hbm": plane_upper,
        "wl_hbm": weight_lower,
        "wu_hbm": weight_upper,
        "cone_hbm": cone_grad,
        "weight_hbm": conv_weight,
        "h_hbm": hidden_field.reshape(ch, depth, nx, ny),
    }
    chunk = (halves, nslab, depth, rows, ny)
    scratch = {n: pltpu.SMEM((depth,), jnp.int32) for n in ("bl", "bu", "plo", "pup", "wl", "wu")}
    scratch["cone"] = pltpu.VMEM(cone_grad.shape, F32)
    scratch["weight"] = pltpu.VMEM(conv_weight.shape, BF16)
    scratch["hbuf"] = pltpu.VMEM((ch, depth, nx, ny), BF16)
    scratch["own"] = pltpu.VMEM(chunk, F32)
    for n in ("z_up", "z_dn", "from_above", "from_below"):
        scratch[n] = pltpu.VMEM(chunk, BF16)
    for h in range(halves):
        scratch["send_a%d" % h] = pltpu.VMEM(chunk[1:], BF16)
        scratch["recv_a%d" % h] = pltpu.VMEM((nz + depth + 2, rows, ny), BF16)
        scratch["send_b%d" % h] = pltpu.VMEM((nslab, depth + 2, rows, ny), BF16)
        scratch["recv_b%d" % h] = pltpu.VMEM((nslab, depth + 2, rows, ny), BF16)
    part = nx // halves
    scratch["shifted"] = pltpu.VMEM((halves, ny // CHUNK, depth * part, 3 * ch * CHUNK), BF16)
    scratch["product"] = pltpu.VMEM((3 * (CHUNK + 2 * EDGE), 3 * ch * CHUNK), F32)
    scratch["wide"] = pltpu.VMEM((27, ch, ny), F32)
    scratch["wmat"] = pltpu.VMEM((ch // 2, 9 * ny, 2 * ny), BF16)
    scratch["lmat"] = pltpu.VMEM((depth * nx, 9 * ny), BF16)
    for n in ("ft0", "ft1"):
        scratch[n] = pltpu.VMEM((ny + 2 * EDGE, (depth + 2) * part), BF16)
    scratch["msg"] = pltpu.VMEM((ch // 4, 128), F32)
    scratch["terms"] = pltpu.VMEM((nbox * nslab, ch // 4, 128), F32)
    scratch["isem"] = dma((7,))
    scratch["csem"] = dma((halves,))
    scratch["hsem"] = dma((1,))
    for n in ("up", "dn"):
        scratch[n + "_s"] = dma((1,))
        scratch[n + "_r"] = dma((halves, nslab // 2))
    for n in ("a", "b"):
        scratch[n + "_s"] = dma((halves,))
        scratch[n + "_r"] = dma((halves,))
    scratch["r_s"] = dma((1,))
    scratch["r_r"] = dma((1,))
    names = (*ins, "out", "wg", *scratch)
    hidden_grad, weight_grad = pl.pallas_call(
        functools.partial(kernel, nbox, nslab, scale, names),
        out_shape=(
            pltpu.VMEM((ch, depth, nx, ny), BF16),
            pltpu.VMEM((ch, 27), F32),
        ),
        in_specs=[hbm] * len(ins),
        out_specs=(vmem, vmem),
        scratch_shapes=list(scratch.values()),
        compiler_params=pltpu.CompilerParams(
            collective_id=0, has_side_effects=True, vmem_limit_bytes=int(44 * 2**20)
        ),
    )(*(pltpu.with_memory_space_constraint(x, pltpu.HBM) for x in ins.values()))
    hidden_grad, weight_grad = pl.pallas_call(
        write,
        out_shape=(pltpu.HBM(hidden_grad.shape, BF16), pltpu.HBM(weight_grad.shape, F32)),
        in_specs=[vmem, vmem],
        out_specs=(hbm, hbm),
        scratch_shapes=[dma((2,))],
    )(pltpu.with_memory_space_constraint(hidden_grad, pltpu.VMEM), pltpu.with_memory_space_constraint(weight_grad, pltpu.VMEM))
    return hidden_grad.reshape(hidden_field.shape), weight_grad


def solution(mesh):
    in_specs = (
        P("box", None, "slab", None, None),
        P(("box", "slab"), None, None),
        P(),
        P(("box", "slab")),
        P(("box", "slab")),
        P(("box", "slab")),
        P(("box", "slab")),
        P(("box", "slab")),
        P(("box", "slab")),
    )
    out_specs = (P("box", None, "slab", None, None), P())
    return jax.shard_map(
        functools.partial(local, mesh.shape["box"], mesh.shape["slab"]),
        mesh=mesh,
        in_specs=in_specs,
        out_specs=out_specs,
        check_vma=False,
    )
```

```python
import functools
import math

import jax
import jax.numpy as jnp
from jax import lax
from jax.experimental import pallas as pl
from jax.experimental.pallas import tpu as pltpu
from jax.sharding import PartitionSpec as P

WDEN = 256
MESH = pl.DeviceIdType.MESH
F32 = jnp.float32
BF16 = jnp.bfloat16
CHUNK = 32
EDGE = 8


def split(nx, nslab):
    rows = nx // nslab
    halves = 2 if rows % 16 == 0 else 1
    return halves, rows // halves


def other(at, j, size):
    bit, partner = 1, at
    while bit < size:
        if j & bit:
            partner = partner + bit * (1 - 2 * lax.rem(lax.div(at, bit), 2))
        bit *= 2
    return partner


def kernel(nbox, nslab, scale, names, *refs):
    r = dict(zip(names, refs, strict=True))
    cone, weight, hbuf, out, wg = r["cone"], r["weight"], r["hbuf"], r["out"], r["wg"]
    bl, bu, plo, pup, wl, wu = (r[n] for n in ("bl", "bu", "plo", "pup", "wl", "wu"))
    own, to_z, from_z = r["own"], r["to_z"], r["from_z"]
    shifted, wide, wmat, lmat, product = r["shifted"], r["wide"], r["wmat"], r["lmat"], r["product"]
    msg, terms = r["msg"], r["terms"]

    g = lax.axis_index("box")
    me = lax.axis_index("slab")
    depth, nx, ny = cone.shape
    halves, rows = split(nx, nslab)
    part = nx // halves
    nz = depth * nslab
    ch = hbuf.shape[0]
    pairs = ch // 2
    chunks = ny // CHUNK
    window = CHUNK + 2 * EDGE
    wide_n = ch * CHUNK
    send_a, send_b = r["send_a"], r["send_b"]
    recv_a = [r["recv_a%d" % h] for h in range(halves)]
    recv_b = [r["recv_b%d" % h] for h in range(halves)]

    smalls = [
        pltpu.make_async_copy(r[n + "_hbm"], r[n], r["isem"].at[i])
        for i, n in enumerate(("bl", "bu", "wl", "wu", "plo", "pup", "weight"))
    ]
    planes = [
        pltpu.make_async_copy(
            r["cone_hbm"].at[:, h * part : (h + 1) * part],
            cone.at[:, h * part : (h + 1) * part],
            r["csem"].at[h],
        )
        for h in range(halves)
    ]
    h_copy = pltpu.make_async_copy(r["h_hbm"], hbuf, r["hsem"].at[0])
    planes[0].start()
    for load in smalls:
        load.start()
    for load in planes[1:]:
        load.start()
    h_copy.start()

    barrier = pltpu.get_barrier_semaphore()

    def greet_slab(j, _):
        pl.semaphore_signal(barrier, inc=1, device_id={"slab": lax.rem(me + j, nslab)}, device_id_type=MESH)
        return 0

    def greet_box(j, _):
        pl.semaphore_signal(barrier, inc=1, device_id={"box": lax.rem(g + j, nbox)}, device_id_type=MESH)
        return 0

    lax.fori_loop(1, nslab, greet_slab, 0)
    lax.fori_loop(1, nbox, greet_box, 0)

    def weigh(h):
        for i in range(depth):
            below_c = jnp.where(bl[i] == g - 1, wl[i].astype(F32) * (1.0 / WDEN), 0.0)
            above_c = jnp.where(bu[i] == g + 1, wu[i].astype(F32) * (1.0 / WDEN), 0.0)
            plane = cone[i, h * part : (h + 1) * part].reshape(nslab, rows, ny)
            to_z[0, h, :, i] = (above_c * plane).astype(BF16)
            to_z[1, h, :, i] = (below_c * plane).astype(BF16)

    def weigh_own(i, _):
        lower = wl[i].astype(F32) * (1.0 / WDEN)
        upper = wu[i].astype(F32) * (1.0 / WDEN)
        own_c = jnp.where(bl[i] == g, lower, 0.0) + jnp.where(bu[i] == g, upper, 0.0)
        own[:, :, i] = own_c * cone[i].reshape(halves, nslab, rows, ny)
        return 0

    def every(source, target, send, recv, at):
        return pltpu.make_async_remote_copy(
            src_ref=source,
            dst_ref=target,
            send_sem=send.at[0],
            recv_sem=recv.at[at],
            device_id={"slab": me},
            device_id_type=MESH,
        )

    def z_copy(way, h, c):
        return pltpu.make_async_remote_copy(
            src_ref=to_z.at[way, h, pl.ds(2 * c, 2)],
            dst_ref=from_z.at[h, c, way],
            send_sem=r["z_s"].at[0],
            recv_sem=r["z_r"].at[h, c],
            device_id={"box": lax.rem(g + (1 if way == 0 else nbox - 1), nbox)},
            device_id_type=MESH,
        )

    inner = jnp.logical_and(g > 0, g < nbox - 1)

    chips = [other(lax.div(me, 2), j, nslab // 2) for j in reversed(range(nslab // 2))]

    def send_z(h, which):
        for c in which:

            @pl.when(g < nbox - 1)
            def _():
                z_copy(0, h, c).start()

            @pl.when(g > 0)
            def _():
                z_copy(1, h, c).start()

    def a_copy(h, t, source):
        return pltpu.make_async_remote_copy(
            src_ref=send_a.at[h, t],
            dst_ref=recv_a[h].at[pl.ds(source * depth, depth)],
            send_sem=r["a_s"].at[0],
            recv_sem=r["a_r"].at[h],
            device_id={"slab": t},
            device_id_type=MESH,
        )

    def merge_send(h, which):
        sibling = other(me, 1, nslab)
        for n, c in which:

            both = from_z.at[h, c]

            @pl.when(inner)
            def _():
                every(both, both, r["z_s"], r["z_r"], (h, c)).wait_recv()

            @pl.when(jnp.logical_not(inner))
            def _():
                every(both.at[0], both.at[0], r["z_s"], r["z_r"], (h, c)).wait_recv()

            def merged(t, at):
                moved_in = from_z[h, c, 0, at].astype(F32) + from_z[h, c, 1, at].astype(F32)
                return (own[h, t] + moved_in).astype(BF16)

            if n < len(chips) - 1:
                for i in range(2):
                    send_a[h, 2 * c + i] = merged(2 * c + i, i)
                    a_copy(h, 2 * c + i, me).start()
            else:
                send_a[h, sibling] = merged(sibling, sibling - 2 * c)
                a_copy(h, sibling, me).start()
                recv_a[h][pl.ds(me * depth, depth)] = merged(me, me - 2 * c)
    def wait_a(h):
        every(send_a.at[h, : nslab - 1], recv_a[h].at[: (nslab - 1) * depth], r["a_s"], r["a_r"], h).wait_recv()

    def b_copy(h, s, source):
        return pltpu.make_async_remote_copy(
            src_ref=send_b.at[h, s],
            dst_ref=recv_b[h].at[source],
            send_sem=r["b_s"].at[0],
            recv_sem=r["b_r"].at[h],
            device_id={"slab": s},
            device_id_type=MESH,
        )

    def turn_send(h):
        offset = jnp.where(bl[0] == g, plo[0], pup[0]) - me * depth

        recv_a[h][nz:] = recv_a[h][: depth + 2]

        def wanted(s):
            return recv_a[h][pl.ds(lax.rem(s * depth - 1 - offset + 2 * nz, nz), depth + 2)]

        for j in reversed(range(1, nslab)):
            s = other(me, j, nslab)
            send_b[h, s] = wanted(s)
            b_copy(h, s, me).start()
        recv_b[h][me] = wanted(me)

    def wait_b(h):
        every(send_b.at[h, : nslab - 1], recv_b[h].at[: nslab - 1], r["b_s"], r["b_r"], h).wait_recv()

    def shift(z, _):
        turned = [hbuf[c, z].T for c in range(ch)]
        for q in range(chunks):
            lanes = jnp.concatenate([t[q * CHUNK : (q + 1) * CHUNK] for t in turned], axis=0).T.astype(F32)
            for dx in (-1, 0, 1):
                rolled = (lanes if dx == 0 else pltpu.roll(lanes, -dx % nx, 0)).astype(BF16)
                for h in range(halves):
                    shifted[
                        h, q, pl.ds(pl.multiple_of(z * part, part), part), (dx + 1) * wide_n : (dx + 2) * wide_n
                    ] = rolled[h * part : (h + 1) * part]
        return 0

    def turn_field(h):
        for p in range(depth + 2):
            if part % 128 == 0:
                turned, at, ft = recv_b[h][:, p].astype(F32).reshape(part, ny).astype(BF16).T, p * part, r["ft0"]
            elif p <= depth:
                two = [recv_b[h][:, p + i].astype(F32).reshape(part, ny) for i in range(2)]
                turned = jnp.concatenate(two, axis=0).astype(BF16).T
                at, ft = (p - p % 2) * part, r["ft%d" % (p % 2)]
            else:
                continue
            at = slice(at, at + turned.shape[1])
            ft[EDGE : EDGE + ny, at] = turned
            ft[0:EDGE, at] = turned[ny - EDGE : ny]
            ft[EDGE + ny : EDGE + ny + EDGE, at] = turned[0:EDGE]

    def planes_from(p, q):
        odd = 0 if part % 128 == 0 else p % 2
        return r["ft%d" % odd][q * CHUNK : q * CHUNK + window, (p - odd) * part : (p - odd + depth) * part]

    def part_product(h):
        turn_field(h)
        total = None
        for q in range(chunks):
            field = jnp.concatenate([planes_from(1 - dz, q) for dz in (-1, 0, 1)], axis=0)
            term = jnp.dot(field, shifted[h, q], preferred_element_type=F32)
            total = term if total is None else total + term
        return total

    def fill_taps():
        y_in = lax.broadcasted_iota(jnp.int32, (ny, ny), 0)
        y_out = lax.broadcasted_iota(jnp.int32, (ny, ny), 1)
        hits = [y_in == lax.rem(y_out - dy + ny, ny) for dy in (-1, 0, 1)]
        taps = weight[...].astype(F32)
        for k in range(27):
            wide[k] = jnp.broadcast_to(taps[:, k : k + 1], (ch, ny))

        def one(p, _):
            for cc in range(2):
                for j in range(9):
                    block = jnp.zeros((ny, ny), F32)
                    for d in range(3):
                        block = jnp.where(hits[d], wide[3 * j + d, pl.ds(2 * p + cc, 1)], block)
                    wmat[p, j * ny : (j + 1) * ny, cc * ny : (cc + 1) * ny] = block.astype(BF16)
            return 0

        lax.fori_loop(0, pairs, one, 0)

    for load in smalls:
        load.wait()
    planes[0].wait()
    weigh(0)
    pl.semaphore_wait(barrier, nslab - 1 + nbox - 1)
    send_z(0, chips[:-1])
    for h in range(1, halves):
        planes[h].wait()
        weigh(h)
        send_z(h, chips[:-1])
    for h in range(halves):
        send_z(h, chips[-1:])

    lax.fori_loop(0, depth, weigh_own, 0)

    @pl.when(g == nbox - 1)
    def _():
        from_z[:, :, 1] = jnp.zeros_like(from_z[:, :, 1])

    @pl.when(g == 0)
    def _():
        from_z[:, :, 0] = jnp.zeros_like(from_z[:, :, 0])

    fill_taps()
    h_copy.wait()
    lax.fori_loop(0, depth // 2, shift, 0)
    order = list(enumerate(chips))
    merge_send(0, order[:-1])
    for h in range(1, halves):
        merge_send(h, order[:-1])
    for h in range(halves):
        merge_send(h, order[-1:])
    for h in range(halves - 1):
        wait_a(h)
        turn_send(h)
    wait_a(halves - 1)
    turn_send(halves - 1)
    lax.fori_loop(depth // 2, depth, shift, 0)
    for h in range(halves - 1):
        wait_b(h)
        product[...] = part_product(h) if h == 0 else product[...] + part_product(h)
    wait_b(halves - 1)
    sums = part_product(halves - 1)
    if halves > 1:
        sums = sums + product[...]
    sums = sums.reshape(3, window, 3 * wide_n)

    def moved(q, dx):
        plane = jnp.concatenate([recv_b[h][:, q].astype(F32).reshape(part, ny) for h in range(halves)], axis=0)
        return (plane if dx == 0 else pltpu.roll(plane, dx % nx, 0)).astype(BF16)

    w_row = lax.broadcasted_iota(jnp.int32, (window, 3 * wide_n), 0)
    w_y = lax.rem(lax.broadcasted_iota(jnp.int32, (window, 3 * wide_n), 1), CHUNK)
    picks = [w_row == w_y + EDGE - dy for dy in (-1, 0, 1)]
    by_tap = []
    for z in range(3):
        by_tap += [jnp.sum(jnp.where(pick, sums[z], 0.0), axis=0, keepdims=True) for pick in picks]
        by_tap.append(jnp.zeros((6 if z < 2 else 11, 3 * wide_n), F32))
    by_tap = jnp.sum(jnp.concatenate(by_tap, axis=0).T.reshape(3, ch, CHUNK, 32), axis=2)
    by_tap = jnp.concatenate([by_tap, jnp.zeros((3, ch, 96), F32)], axis=2)
    by_channel = by_tap[0] + pltpu.roll(by_tap[1], 3, 1) + pltpu.roll(by_tap[2], 6, 1)
    of_four = lax.rem(lax.broadcasted_iota(jnp.int32, (ch, 128), 0), 4)
    packed = jnp.where(of_four == 0, by_channel, 0.0)
    for i in range(1, 4):
        packed = packed + pltpu.roll(jnp.where(of_four == i, by_channel, 0.0), 32 * i, 1)
    packed = jnp.sum(packed.reshape(ch // 4, 4, 128), axis=1)
    ndev = nbox * nslab
    my = g * nslab + me
    msg[...] = packed
    terms[my] = packed

    def r_copy(b, s, source):
        return pltpu.make_async_remote_copy(
            src_ref=msg,
            dst_ref=terms.at[source],
            send_sem=r["r_s"].at[0],
            recv_sem=r["r_r"].at[0],
            device_id={"box": b, "slab": s},
            device_id_type=MESH,
        )

    def send_r():
        for j in reversed(range(1, ndev)):
            r_copy(other(g, j // nslab, nbox), other(me, j % nslab, nslab), my).start()

    def pair_grads(p, _):
        grads = jnp.dot(lmat[...], wmat[p], preferred_element_type=F32)
        for cc in range(2):
            out[2 * p + cc] = grads[:, cc * ny : (cc + 1) * ny].reshape(depth, nx, ny).astype(BF16)
        return 0

    send_r()
    for q in range(depth + 2):
        for dx in (-1, 0, 1):
            plane = moved(q, dx)
            for dz in (-1, 0, 1):
                z, j = q + dz - 1, (dz + 1) * 3 + dx + 1
                if 0 <= z < depth:
                    lmat[z * nx : (z + 1) * nx, j * ny : (j + 1) * ny] = plane
    lax.fori_loop(0, pairs, pair_grads, 0)

    @pl.when(inner)
    def _():
        every(to_z, to_z, r["z_s"], r["z_s"], 0).wait_send()

    @pl.when(jnp.logical_not(inner))
    def _():
        every(to_z.at[0], to_z.at[0], r["z_s"], r["z_s"], 0).wait_send()

    a_sent, b_sent = send_a.at[:, : nslab - 1], send_b.at[:, : nslab - 1]
    every(a_sent, a_sent, r["a_s"], r["a_s"], 0).wait_send()
    every(b_sent, b_sent, r["b_s"], r["b_s"], 0).wait_send()
    r_all = every(terms.at[: ndev - 1], terms.at[: ndev - 1], r["r_s"], r["r_r"], 0)
    r_all.wait_send()
    r_all.wait_recv()
    total = jnp.sum(terms[...], axis=0) * scale
    for c in range(ch):
        wg[c : c + 1, :] = total[c // 4 : c // 4 + 1, (c % 4) * 32 : (c % 4) * 32 + 27]


def write(grads, terms, out, wg, sem):
    copies = [pltpu.make_async_copy(terms, wg, sem.at[0]), pltpu.make_async_copy(grads, out, sem.at[1])]
    for copy in copies:
        copy.start()
    for copy in copies:
        copy.wait()


def local(
    nbox,
    nslab,
    hidden_field,
    cone_grad,
    conv_weight,
    box_lower,
    box_upper,
    plane_lower,
    plane_upper,
    weight_lower,
    weight_upper,
):
    _, ch, depth, nx, ny = hidden_field.shape
    halves, rows = split(nx, nslab)
    nz = depth * nslab
    scale = 1.0 / math.sqrt(nbox * nz * nx * ny)
    vmem = pl.BlockSpec(memory_space=pltpu.VMEM)
    hbm = pl.BlockSpec(memory_space=pltpu.HBM)
    dma = pltpu.SemaphoreType.DMA
    ins = {
        "bl_hbm": box_lower,
        "bu_hbm": box_upper,
        "plo_hbm": plane_lower,
        "pup_hbm": plane_upper,
        "wl_hbm": weight_lower,
        "wu_hbm": weight_upper,
        "cone_hbm": cone_grad,
        "weight_hbm": conv_weight,
        "h_hbm": hidden_field.reshape(ch, depth, nx, ny),
    }
    chunk = (halves, nslab, depth, rows, ny)
    scratch = {n: pltpu.SMEM((depth,), jnp.int32) for n in ("bl", "bu", "plo", "pup", "wl", "wu")}
    scratch["cone"] = pltpu.VMEM(cone_grad.shape, F32)
    scratch["weight"] = pltpu.VMEM(conv_weight.shape, BF16)
    scratch["hbuf"] = pltpu.VMEM((ch, depth, nx, ny), BF16)
    scratch["own"] = pltpu.VMEM(chunk, F32)
    scratch["to_z"] = pltpu.VMEM((2, *chunk), BF16)
    scratch["from_z"] = pltpu.VMEM((halves, nslab // 2, 2, 2, depth, rows, ny), BF16)
    scratch["send_a"] = pltpu.VMEM(chunk, BF16)
    scratch["send_b"] = pltpu.VMEM((halves, nslab, depth + 2, rows, ny), BF16)
    for h in range(halves):
        scratch["recv_a%d" % h] = pltpu.VMEM((nz + depth + 2, rows, ny), BF16)
        scratch["recv_b%d" % h] = pltpu.VMEM((nslab, depth + 2, rows, ny), BF16)
    part = nx // halves
    scratch["shifted"] = pltpu.VMEM((halves, ny // CHUNK, depth * part, 3 * ch * CHUNK), BF16)
    scratch["product"] = pltpu.VMEM((3 * (CHUNK + 2 * EDGE), 3 * ch * CHUNK), F32)
    scratch["wide"] = pltpu.VMEM((27, ch, ny), F32)
    scratch["wmat"] = pltpu.VMEM((ch // 2, 9 * ny, 2 * ny), BF16)
    scratch["lmat"] = pltpu.VMEM((depth * nx, 9 * ny), BF16)
    for n in ("ft0", "ft1"):
        scratch[n] = pltpu.VMEM((ny + 2 * EDGE, (depth + 2) * part), BF16)
    scratch["msg"] = pltpu.VMEM((ch // 4, 128), F32)
    scratch["terms"] = pltpu.VMEM((nbox * nslab, ch // 4, 128), F32)
    scratch["isem"] = dma((7,))
    scratch["csem"] = dma((halves,))
    scratch["hsem"] = dma((1,))
    scratch["z_s"] = dma((1,))
    scratch["z_r"] = dma((halves, nslab // 2))
    for n in ("a", "b"):
        scratch[n + "_s"] = dma((1,))
        scratch[n + "_r"] = dma((halves,))
    scratch["r_s"] = dma((1,))
    scratch["r_r"] = dma((1,))
    names = (*ins, "out", "wg", *scratch)
    hidden_grad, weight_grad = pl.pallas_call(
        functools.partial(kernel, nbox, nslab, scale, names),
        out_shape=(
            pltpu.VMEM((ch, depth, nx, ny), BF16),
            pltpu.VMEM((ch, 27), F32),
        ),
        in_specs=[hbm] * len(ins),
        out_specs=(vmem, vmem),
        scratch_shapes=list(scratch.values()),
        compiler_params=pltpu.CompilerParams(
            collective_id=0, has_side_effects=True, vmem_limit_bytes=int(44 * 2**20)
        ),
    )(*(pltpu.with_memory_space_constraint(x, pltpu.HBM) for x in ins.values()))
    hidden_grad, weight_grad = pl.pallas_call(
        write,
        out_shape=(pltpu.HBM(hidden_grad.shape, BF16), pltpu.HBM(weight_grad.shape, F32)),
        in_specs=[vmem, vmem],
        out_specs=(hbm, hbm),
        scratch_shapes=[dma((2,))],
    )(pltpu.with_memory_space_constraint(hidden_grad, pltpu.VMEM), pltpu.with_memory_space_constraint(weight_grad, pltpu.VMEM))
    return hidden_grad.reshape(hidden_field.shape), weight_grad


def solution(mesh):
    in_specs = (
        P("box", None, "slab", None, None),
        P(("box", "slab"), None, None),
        P(),
        P(("box", "slab")),
        P(("box", "slab")),
        P(("box", "slab")),
        P(("box", "slab")),
        P(("box", "slab")),
        P(("box", "slab")),
    )
    out_specs = (P("box", None, "slab", None, None), P())
    return jax.shard_map(
        functools.partial(local, mesh.shape["box"], mesh.shape["slab"]),
        mesh=mesh,
        in_specs=in_specs,
        out_specs=out_specs,
        check_vma=False,
    )
```

```python
import functools
import math

import jax
import jax.numpy as jnp
from jax import lax
from jax.experimental import pallas as pl
from jax.experimental.pallas import tpu as pltpu
from jax.sharding import PartitionSpec as P

WDEN = 256
MESH = pl.DeviceIdType.MESH
F32 = jnp.float32
BF16 = jnp.bfloat16
CHUNK = 32
EDGE = 8


def split(nx, nslab):
    rows = nx // nslab
    halves = 2 if rows % 16 == 0 else 1
    return halves, rows // halves


def other(at, j, size):
    bit, partner = 1, at
    while bit < size:
        if j & bit:
            partner = partner + bit * (1 - 2 * lax.rem(lax.div(at, bit), 2))
        bit *= 2
    return partner


def kernel(nbox, nslab, scale, names, *refs):
    r = dict(zip(names, refs, strict=True))
    cone, weight, hbuf, out, wg = r["cone"], r["weight"], r["hbuf"], r["out"], r["wg"]
    bl, bu, plo, pup, wl, wu = (r[n] for n in ("bl", "bu", "plo", "pup", "wl", "wu"))
    own, to_z, from_z = r["own"], r["to_z"], r["from_z"]
    shifted, wide, wmat, lmat, product = r["shifted"], r["wide"], r["wmat"], r["lmat"], r["product"]
    msg, terms = r["msg"], r["terms"]

    g = lax.axis_index("box")
    me = lax.axis_index("slab")
    depth, nx, ny = cone.shape
    halves, rows = split(nx, nslab)
    part = nx // halves
    nz = depth * nslab
    ch = hbuf.shape[0]
    pairs = ch // 2
    chunks = ny // CHUNK
    window = CHUNK + 2 * EDGE
    wide_n = ch * CHUNK
    send_a, send_b = r["send_a"], r["send_b"]
    recv_a = [r["recv_a%d" % h] for h in range(halves)]
    recv_b = [r["recv_b%d" % h] for h in range(halves)]

    smalls = [
        pltpu.make_async_copy(r[n + "_hbm"], r[n], r["isem"].at[i])
        for i, n in enumerate(("bl", "bu", "wl", "wu", "plo", "pup", "weight"))
    ]
    planes = [
        pltpu.make_async_copy(
            r["cone_hbm"].at[:, h * part : (h + 1) * part],
            cone.at[:, h * part : (h + 1) * part],
            r["csem"].at[h],
        )
        for h in range(halves)
    ]
    h_copy = pltpu.make_async_copy(r["h_hbm"], hbuf, r["hsem"].at[0])
    planes[0].start()
    for load in smalls:
        load.start()
    for load in planes[1:]:
        load.start()
    h_copy.start()

    barrier = pltpu.get_barrier_semaphore()

    def greet_slab(j, _):
        pl.semaphore_signal(barrier, inc=1, device_id={"slab": lax.rem(me + j, nslab)}, device_id_type=MESH)
        return 0

    def greet_box(j, _):
        pl.semaphore_signal(barrier, inc=1, device_id={"box": lax.rem(g + j, nbox)}, device_id_type=MESH)
        return 0

    lax.fori_loop(1, nslab, greet_slab, 0)
    lax.fori_loop(1, nbox, greet_box, 0)

    def weigh(h):
        for i in range(depth):
            below_c = jnp.where(bl[i] == g - 1, wl[i].astype(F32) * (1.0 / WDEN), 0.0)
            above_c = jnp.where(bu[i] == g + 1, wu[i].astype(F32) * (1.0 / WDEN), 0.0)
            plane = cone[i, h * part : (h + 1) * part].reshape(nslab, rows, ny)
            to_z[0, h, :, i] = (above_c * plane).astype(BF16)
            to_z[1, h, :, i] = (below_c * plane).astype(BF16)

    def weigh_own(i, _):
        lower = wl[i].astype(F32) * (1.0 / WDEN)
        upper = wu[i].astype(F32) * (1.0 / WDEN)
        own_c = jnp.where(bl[i] == g, lower, 0.0) + jnp.where(bu[i] == g, upper, 0.0)
        own[:, :, i] = own_c * cone[i].reshape(halves, nslab, rows, ny)
        return 0

    def every(source, target, send, recv, at):
        return pltpu.make_async_remote_copy(
            src_ref=source,
            dst_ref=target,
            send_sem=send.at[0],
            recv_sem=recv.at[at],
            device_id={"slab": me},
            device_id_type=MESH,
        )

    def z_copy(way, h, c):
        return pltpu.make_async_remote_copy(
            src_ref=to_z.at[way, h, pl.ds(2 * c, 2)],
            dst_ref=from_z.at[h, c, way],
            send_sem=r["z_s"].at[0],
            recv_sem=r["z_r"].at[h, c],
            device_id={"box": lax.rem(g + (1 if way == 0 else nbox - 1), nbox)},
            device_id_type=MESH,
        )

    inner = jnp.logical_and(g > 0, g < nbox - 1)

    chips = [other(lax.div(me, 2), j, nslab // 2) for j in reversed(range(nslab // 2))]

    def send_z(h, which):
        for c in which:

            @pl.when(g < nbox - 1)
            def _():
                z_copy(0, h, c).start()

            @pl.when(g > 0)
            def _():
                z_copy(1, h, c).start()

    def a_copy(h, t, source):
        return pltpu.make_async_remote_copy(
            src_ref=send_a.at[h, t],
            dst_ref=recv_a[h].at[pl.ds(source * depth, depth)],
            send_sem=r["a_s"].at[0],
            recv_sem=r["a_r"].at[h],
            device_id={"slab": t},
            device_id_type=MESH,
        )

    def merge_send(h, which):
        sibling = other(me, 1, nslab)
        for n, c in which:

            both = from_z.at[h, c]

            @pl.when(inner)
            def _():
                every(both, both, r["z_s"], r["z_r"], (h, c)).wait_recv()

            @pl.when(jnp.logical_not(inner))
            def _():
                every(both.at[0], both.at[0], r["z_s"], r["z_r"], (h, c)).wait_recv()

            def merged(t, at):
                moved_in = from_z[h, c, 0, at].astype(F32) + from_z[h, c, 1, at].astype(F32)
                return (own[h, t] + moved_in).astype(BF16)

            if n < len(chips) - 1:
                for i in range(2):
                    send_a[h, 2 * c + i] = merged(2 * c + i, i)
                    a_copy(h, 2 * c + i, me).start()
            else:
                send_a[h, sibling] = merged(sibling, sibling - 2 * c)
                a_copy(h, sibling, me).start()
                recv_a[h][pl.ds(me * depth, depth)] = merged(me, me - 2 * c)
    def wait_a(h):
        every(send_a.at[h, : nslab - 1], recv_a[h].at[: (nslab - 1) * depth], r["a_s"], r["a_r"], h).wait_recv()

    def b_copy(h, s, source):
        return pltpu.make_async_remote_copy(
            src_ref=send_b.at[h, s],
            dst_ref=recv_b[h].at[source],
            send_sem=r["b_s"].at[0],
            recv_sem=r["b_r"].at[h],
            device_id={"slab": s},
            device_id_type=MESH,
        )

    def turn_send(h):
        offset = jnp.where(bl[0] == g, plo[0], pup[0]) - me * depth

        recv_a[h][nz:] = recv_a[h][: depth + 2]

        def wanted(s):
            return recv_a[h][pl.ds(lax.rem(s * depth - 1 - offset + 2 * nz, nz), depth + 2)]

        for j in sorted(range(1, nslab), key=lambda j: (-(j // 2).bit_count(), j % 2, j)):
            s = other(me, j, nslab)
            send_b[h, s] = wanted(s)
            b_copy(h, s, me).start()
        recv_b[h][me] = wanted(me)

    def wait_b(h):
        every(send_b.at[h, : nslab - 1], recv_b[h].at[: nslab - 1], r["b_s"], r["b_r"], h).wait_recv()

    def shift(z, _):
        turned = [hbuf[c, z].T for c in range(ch)]
        for q in range(chunks):
            lanes = jnp.concatenate([t[q * CHUNK : (q + 1) * CHUNK] for t in turned], axis=0).T.astype(F32)
            for dx in (-1, 0, 1):
                rolled = (lanes if dx == 0 else pltpu.roll(lanes, -dx % nx, 0)).astype(BF16)
                for h in range(halves):
                    shifted[
                        h, q, pl.ds(pl.multiple_of(z * part, part), part), (dx + 1) * wide_n : (dx + 2) * wide_n
                    ] = rolled[h * part : (h + 1) * part]
        return 0

    def turn_field(h):
        for p in range(depth + 2):
            if part % 128 == 0:
                turned, at, ft = recv_b[h][:, p].astype(F32).reshape(part, ny).astype(BF16).T, p * part, r["ft0"]
            elif p <= depth:
                two = [recv_b[h][:, p + i].astype(F32).reshape(part, ny) for i in range(2)]
                turned = jnp.concatenate(two, axis=0).astype(BF16).T
                at, ft = (p - p % 2) * part, r["ft%d" % (p % 2)]
            else:
                continue
            at = slice(at, at + turned.shape[1])
            ft[EDGE : EDGE + ny, at] = turned
            ft[0:EDGE, at] = turned[ny - EDGE : ny]
            ft[EDGE + ny : EDGE + ny + EDGE, at] = turned[0:EDGE]

    def planes_from(p, q):
        odd = 0 if part % 128 == 0 else p % 2
        return r["ft%d" % odd][q * CHUNK : q * CHUNK + window, (p - odd) * part : (p - odd + depth) * part]

    def part_product(h):
        turn_field(h)
        total = None
        for q in range(chunks):
            field = jnp.concatenate([planes_from(1 - dz, q) for dz in (-1, 0, 1)], axis=0)
            term = jnp.dot(field, shifted[h, q], preferred_element_type=F32)
            total = term if total is None else total + term
        return total

    def fill_taps():
        y_in = lax.broadcasted_iota(jnp.int32, (ny, ny), 0)
        y_out = lax.broadcasted_iota(jnp.int32, (ny, ny), 1)
        hits = [y_in == lax.rem(y_out - dy + ny, ny) for dy in (-1, 0, 1)]
        taps = weight[...].astype(F32)
        for k in range(27):
            wide[k] = jnp.broadcast_to(taps[:, k : k + 1], (ch, ny))

        def one(p, _):
            for cc in range(2):
                for j in range(9):
                    block = jnp.zeros((ny, ny), F32)
                    for d in range(3):
                        block = jnp.where(hits[d], wide[3 * j + d, pl.ds(2 * p + cc, 1)], block)
                    wmat[p, j * ny : (j + 1) * ny, cc * ny : (cc + 1) * ny] = block.astype(BF16)
            return 0

        lax.fori_loop(0, pairs, one, 0)

    for load in smalls:
        load.wait()
    planes[0].wait()
    weigh(0)
    pl.semaphore_wait(barrier, nslab - 1 + nbox - 1)
    send_z(0, chips[:-1])
    for h in range(1, halves):
        planes[h].wait()
        weigh(h)
        send_z(h, chips[:-1])
    for h in range(halves):
        send_z(h, chips[-1:])

    lax.fori_loop(0, depth, weigh_own, 0)

    @pl.when(g == nbox - 1)
    def _():
        from_z[:, :, 1] = jnp.zeros_like(from_z[:, :, 1])

    @pl.when(g == 0)
    def _():
        from_z[:, :, 0] = jnp.zeros_like(from_z[:, :, 0])

    fill_taps()
    h_copy.wait()
    lax.fori_loop(0, depth // 2, shift, 0)
    order = list(enumerate(chips))
    merge_send(0, order[:-1])
    for h in range(1, halves):
        merge_send(h, order[:-1])
    for h in range(halves):
        merge_send(h, order[-1:])
    for h in range(halves - 1):
        wait_a(h)
        turn_send(h)
    wait_a(halves - 1)
    turn_send(halves - 1)
    lax.fori_loop(depth // 2, depth, shift, 0)
    for h in range(halves - 1):
        wait_b(h)
        product[...] = part_product(h) if h == 0 else product[...] + part_product(h)
    wait_b(halves - 1)
    sums = part_product(halves - 1)
    if halves > 1:
        sums = sums + product[...]
    sums = sums.reshape(3, window, 3 * wide_n)

    def moved(q, dx):
        plane = jnp.concatenate([recv_b[h][:, q].astype(F32).reshape(part, ny) for h in range(halves)], axis=0)
        return (plane if dx == 0 else pltpu.roll(plane, dx % nx, 0)).astype(BF16)

    w_row = lax.broadcasted_iota(jnp.int32, (window, 3 * wide_n), 0)
    w_y = lax.rem(lax.broadcasted_iota(jnp.int32, (window, 3 * wide_n), 1), CHUNK)
    picks = [w_row == w_y + EDGE - dy for dy in (-1, 0, 1)]
    by_tap = []
    for z in range(3):
        by_tap += [jnp.sum(jnp.where(pick, sums[z], 0.0), axis=0, keepdims=True) for pick in picks]
        by_tap.append(jnp.zeros((6 if z < 2 else 11, 3 * wide_n), F32))
    by_tap = jnp.sum(jnp.concatenate(by_tap, axis=0).T.reshape(3, ch, CHUNK, 32), axis=2)
    by_tap = jnp.concatenate([by_tap, jnp.zeros((3, ch, 96), F32)], axis=2)
    by_channel = by_tap[0] + pltpu.roll(by_tap[1], 3, 1) + pltpu.roll(by_tap[2], 6, 1)
    of_four = lax.rem(lax.broadcasted_iota(jnp.int32, (ch, 128), 0), 4)
    packed = jnp.where(of_four == 0, by_channel, 0.0)
    for i in range(1, 4):
        packed = packed + pltpu.roll(jnp.where(of_four == i, by_channel, 0.0), 32 * i, 1)
    packed = jnp.sum(packed.reshape(ch // 4, 4, 128), axis=1)
    ndev = nbox * nslab
    my = g * nslab + me
    msg[...] = packed
    terms[my] = packed

    def r_copy(b, s, source):
        return pltpu.make_async_remote_copy(
            src_ref=msg,
            dst_ref=terms.at[source],
            send_sem=r["r_s"].at[0],
            recv_sem=r["r_r"].at[0],
            device_id={"box": b, "slab": s},
            device_id_type=MESH,
        )

    def send_r():
        for j in reversed(range(1, ndev)):
            r_copy(other(g, j // nslab, nbox), other(me, j % nslab, nslab), my).start()

    def pair_grads(p, _):
        grads = jnp.dot(lmat[...], wmat[p], preferred_element_type=F32)
        for cc in range(2):
            out[2 * p + cc] = grads[:, cc * ny : (cc + 1) * ny].reshape(depth, nx, ny).astype(BF16)
        return 0

    send_r()
    for q in range(depth + 2):
        for dx in (-1, 0, 1):
            plane = moved(q, dx)
            for dz in (-1, 0, 1):
                z, j = q + dz - 1, (dz + 1) * 3 + dx + 1
                if 0 <= z < depth:
                    lmat[z * nx : (z + 1) * nx, j * ny : (j + 1) * ny] = plane
    lax.fori_loop(0, pairs, pair_grads, 0)

    @pl.when(inner)
    def _():
        every(to_z, to_z, r["z_s"], r["z_s"], 0).wait_send()

    @pl.when(jnp.logical_not(inner))
    def _():
        every(to_z.at[0], to_z.at[0], r["z_s"], r["z_s"], 0).wait_send()

    a_sent, b_sent = send_a.at[:, : nslab - 1], send_b.at[:, : nslab - 1]
    every(a_sent, a_sent, r["a_s"], r["a_s"], 0).wait_send()
    every(b_sent, b_sent, r["b_s"], r["b_s"], 0).wait_send()
    r_all = every(terms.at[: ndev - 1], terms.at[: ndev - 1], r["r_s"], r["r_r"], 0)
    r_all.wait_send()
    r_all.wait_recv()
    total = jnp.sum(terms[...], axis=0) * scale
    for c in range(ch):
        wg[c : c + 1, :] = total[c // 4 : c // 4 + 1, (c % 4) * 32 : (c % 4) * 32 + 27]


def write(grads, terms, out, wg, sem):
    copies = [pltpu.make_async_copy(terms, wg, sem.at[0]), pltpu.make_async_copy(grads, out, sem.at[1])]
    for copy in copies:
        copy.start()
    for copy in copies:
        copy.wait()


def local(
    nbox,
    nslab,
    hidden_field,
    cone_grad,
    conv_weight,
    box_lower,
    box_upper,
    plane_lower,
    plane_upper,
    weight_lower,
    weight_upper,
):
    _, ch, depth, nx, ny = hidden_field.shape
    halves, rows = split(nx, nslab)
    nz = depth * nslab
    scale = 1.0 / math.sqrt(nbox * nz * nx * ny)
    vmem = pl.BlockSpec(memory_space=pltpu.VMEM)
    hbm = pl.BlockSpec(memory_space=pltpu.HBM)
    dma = pltpu.SemaphoreType.DMA
    ins = {
        "bl_hbm": box_lower,
        "bu_hbm": box_upper,
        "plo_hbm": plane_lower,
        "pup_hbm": plane_upper,
        "wl_hbm": weight_lower,
        "wu_hbm": weight_upper,
        "cone_hbm": cone_grad,
        "weight_hbm": conv_weight,
        "h_hbm": hidden_field.reshape(ch, depth, nx, ny),
    }
    chunk = (halves, nslab, depth, rows, ny)
    scratch = {n: pltpu.SMEM((depth,), jnp.int32) for n in ("bl", "bu", "plo", "pup", "wl", "wu")}
    scratch["cone"] = pltpu.VMEM(cone_grad.shape, F32)
    scratch["weight"] = pltpu.VMEM(conv_weight.shape, BF16)
    scratch["hbuf"] = pltpu.VMEM((ch, depth, nx, ny), BF16)
    scratch["own"] = pltpu.VMEM(chunk, F32)
    scratch["to_z"] = pltpu.VMEM((2, *chunk), BF16)
    scratch["from_z"] = pltpu.VMEM((halves, nslab // 2, 2, 2, depth, rows, ny), BF16)
    scratch["send_a"] = pltpu.VMEM(chunk, BF16)
    scratch["send_b"] = pltpu.VMEM((halves, nslab, depth + 2, rows, ny), BF16)
    for h in range(halves):
        scratch["recv_a%d" % h] = pltpu.VMEM((nz + depth + 2, rows, ny), BF16)
        scratch["recv_b%d" % h] = pltpu.VMEM((nslab, depth + 2, rows, ny), BF16)
    part = nx // halves
    scratch["shifted"] = pltpu.VMEM((halves, ny // CHUNK, depth * part, 3 * ch * CHUNK), BF16)
    scratch["product"] = pltpu.VMEM((3 * (CHUNK + 2 * EDGE), 3 * ch * CHUNK), F32)
    scratch["wide"] = pltpu.VMEM((27, ch, ny), F32)
    scratch["wmat"] = pltpu.VMEM((ch // 2, 9 * ny, 2 * ny), BF16)
    scratch["lmat"] = pltpu.VMEM((depth * nx, 9 * ny), BF16)
    for n in ("ft0", "ft1"):
        scratch[n] = pltpu.VMEM((ny + 2 * EDGE, (depth + 2) * part), BF16)
    scratch["msg"] = pltpu.VMEM((ch // 4, 128), F32)
    scratch["terms"] = pltpu.VMEM((nbox * nslab, ch // 4, 128), F32)
    scratch["isem"] = dma((7,))
    scratch["csem"] = dma((halves,))
    scratch["hsem"] = dma((1,))
    scratch["z_s"] = dma((1,))
    scratch["z_r"] = dma((halves, nslab // 2))
    for n in ("a", "b"):
        scratch[n + "_s"] = dma((1,))
        scratch[n + "_r"] = dma((halves,))
    scratch["r_s"] = dma((1,))
    scratch["r_r"] = dma((1,))
    names = (*ins, "out", "wg", *scratch)
    hidden_grad, weight_grad = pl.pallas_call(
        functools.partial(kernel, nbox, nslab, scale, names),
        out_shape=(
            pltpu.VMEM((ch, depth, nx, ny), BF16),
            pltpu.VMEM((ch, 27), F32),
        ),
        in_specs=[hbm] * len(ins),
        out_specs=(vmem, vmem),
        scratch_shapes=list(scratch.values()),
        compiler_params=pltpu.CompilerParams(
            collective_id=0, has_side_effects=True, vmem_limit_bytes=int(44 * 2**20)
        ),
    )(*(pltpu.with_memory_space_constraint(x, pltpu.HBM) for x in ins.values()))
    hidden_grad, weight_grad = pl.pallas_call(
        write,
        out_shape=(pltpu.HBM(hidden_grad.shape, BF16), pltpu.HBM(weight_grad.shape, F32)),
        in_specs=[vmem, vmem],
        out_specs=(hbm, hbm),
        scratch_shapes=[dma((2,))],
    )(pltpu.with_memory_space_constraint(hidden_grad, pltpu.VMEM), pltpu.with_memory_space_constraint(weight_grad, pltpu.VMEM))
    return hidden_grad.reshape(hidden_field.shape), weight_grad


def solution(mesh):
    in_specs = (
        P("box", None, "slab", None, None),
        P(("box", "slab"), None, None),
        P(),
        P(("box", "slab")),
        P(("box", "slab")),
        P(("box", "slab")),
        P(("box", "slab")),
        P(("box", "slab")),
        P(("box", "slab")),
    )
    out_specs = (P("box", None, "slab", None, None), P())
    return jax.shard_map(
        functools.partial(local, mesh.shape["box"], mesh.shape["slab"]),
        mesh=mesh,
        in_specs=in_specs,
        out_specs=out_specs,
        check_vma=False,
    )
```
